256 devices in a mesh: section: 8 (over x, core), tp: 32 (over y, z).
Axes of the slice: x: 4, y: 4, z: 8, core: 2. Of those that a mesh axis runs over, the one named last changes fastest.
Arguments:
- hidden: bfloat16 [8, 24, 8192], P('section', None, 'tp'), may hold values from -6 to 6
- attention_norm_scale: float32 [8192], replicated, may hold values from 0.1 to 1.9
- joined_projection_weight: bfloat16 [8, 8192, 10240], P('section', None, 'tp'), may hold values from -0.0625 to 0.0625
- adapter_down_weight: bfloat16 [8, 32, 8192, 64], P('section', 'tp'), may hold values from -0.0625 to 0.0625
- adapter_up_weight: bfloat16 [8, 32, 64, 10240], P('section', 'tp'), may hold values from -0.75 to 0.75
- cached_key_rows: bfloat16 [8, 24, 1024, 1024], P('section', None, 'tp'), may hold values from -180 to 180
- cached_value_rows: bfloat16 [8, 24, 1024, 1024], P('section', None, 'tp'), may hold values from -6 to 6
- row_adapter_index: int32 [8, 24, 1], P('section'), may hold values from 0 to 31; in each aligned block of 24 rows (0 to 23, 24 to 47, ..., all dimensions but the last counted through in order) at most 2 rows name the same one
- lengths: int32 [8, 24], P('section'), may hold values from 1 to 1023, 12288 in all within a row
Outputs:
- residual_out: bfloat16 [8, 24, 8192], P('section', None, 'tp')
- context: bfloat16 [8, 24, 8192], P('section', None, 'tp')
The draws below stay inside these ranges and needn't reach their ends.
Inputs may be any that keep to these rules, and one draw needn't show every extreme that they name: `row_adapter_index`: in each section's batch at most 2 rows name the same adapter, a bound that some block reaches. The new token follows the used positions; the 24 lengths of one section's batch sum to 12288, and some row uses 1024 - 1 positions.
All inputs are finite; a program needn't handle non-finite values.
Results may differ from the reference program's by a relative error of at most 0.024.
Values may be sent and summed in bfloat16 or wider, within the bound.
No kernel may reach another device: no remote copies, remote signals or barrier semaphores. Data moves between devices by JAX's collectives and lax.ppermute only.
A program may use at most 128 MiB of HBM per device.

```python
import math
import jax
import jax.numpy as jnp
import numpy as np
from jax import lax

MODEL_WIDTH = 8192
H = 64
KVH = 8
HD = 128
ADAPTER_RANK = 64
CTX = 1024
ROWS = 24
MOST = 2
QD = 8192
KVD = 1024
JOINED_COLUMNS = 10240
ADAPTER_COUNT = 32
N_SECTION = 8


def draw_cached_key_rows(key, part):
    key = jax.random.fold_in(key, 11)
    base = jax.random.truncated_normal(key, -6.0, 6.0, (N_SECTION, ROWS, CTX, KVD), jnp.float32)
    return base.astype(jnp.bfloat16)


def level_of(stream_key, dims, pieces, smallest, top_value):
    gain = 1.0
    for dim, shards_of in pieces:
        draws = jax.random.uniform(jax.random.fold_in(jax.random.fold_in(stream_key, 6), dim), (shards_of,), jnp.float32, smallest / len(pieces), top_value / len(pieces))
        gain = gain * jnp.repeat(jnp.exp(draws), dims[dim] // shards_of).reshape((-1,) + (1,) * (len(dims) - 1 - dim))
    return gain


def split_up(count, total, most, lean):
    weights = [(1 << 20) // math.isqrt(rank ** lean) + 1 for rank in range(2, count + 1)]
    surplus, counts = total - most - (count - 1), [1] * (count - 1)
    while surplus > 0:
        movable = [i for i in range(count - 1) if counts[i] < most]
        mass, remaining = sum([weights[i] for i in movable]), surplus
        for i in movable:
            addition = min(most - counts[i], max(1, remaining * weights[i] // mass), surplus)
            counts[i] = counts[i] + addition
            surplus = surplus - addition
    return np.array([most] + counts)


def ragged_sizes(rng, number_of, total, most, slope):
    if number_of == 2:
        one = jax.random.randint(rng, (), max(1, total - most), min(most, total - 1) + 1)
        return jnp.stack([one, total - one])
    tallies = jnp.asarray(split_up(number_of, total, most, slope), jnp.int32)
    pairs = (number_of - 1) // 2
    donor, sink = tallies[1:1 + 2 * pairs:2], tallies[2:2 + 2 * pairs:2]
    room = jnp.minimum(donor - 1, most - sink)
    moved = jax.random.randint(jax.random.fold_in(rng, 1), (pairs,), 0, 1 << 20) % (room + 1)
    tallies = tallies.at[1:1 + 2 * pairs:2].set(donor - moved).at[2:2 + 2 * pairs:2].set(sink + moved)
    return tallies[jax.random.permutation(jax.random.fold_in(rng, 2), number_of)]


def assign_block(own_key, own, number, rows, count, top, most, slope):
    ranking = jax.random.permutation(own_key, count)
    crowded, ordinary = portions_of(count, rows * top, most, slope, True), portions_of(count, rows * top, most, slope, False)
    places = jnp.arange(count)

    def named(tallies, rotation):
        used = int((tallies > 0).sum())
        fixed = max(1, used // 4)
        shifted = fixed + (places - fixed + rotation * (used - fixed)) % max(1, count - fixed)
        return jnp.zeros((count,), jnp.int32).at[ranking[jnp.where(places < fixed, places, shifted)]].set(jnp.asarray(tallies, jnp.int32))

    tallies = jnp.where(number % 4 == 0, named(crowded, number // 4), named(ordinary, number - number // 4 - 1))
    mixed = jax.random.permutation(jax.random.fold_in(own, 3), count)
    giver, sink = mixed[0:count // 2 * 2:2], mixed[1:count // 2 * 2:2]
    margin = jnp.minimum(tallies[giver] - 1, most - tallies[sink]) // 2
    margin = jnp.where((giver == ranking[0]) | (sink == ranking[0]) | (tallies[sink] == 0), 0, jnp.maximum(margin, 0))
    shifted = jax.random.randint(jax.random.fold_in(own, 4), (count // 2,), 0, 1 << 20) % (margin + 1)
    tallies = tallies.at[giver].add(-shifted).at[sink].add(shifted)
    items = jnp.searchsorted(jnp.cumsum(tallies), jnp.arange(rows * top), side="right").astype(jnp.int32)
    listing = items.reshape(top, rows).T
    listing = listing[jax.random.permutation(jax.random.fold_in(own, 1), rows)]
    rotation = jax.random.randint(jax.random.fold_in(own, 2), (rows, 1), 0, top)
    return jnp.take_along_axis(listing, (jnp.arange(top)[None, :] + rotation) % top, axis=1)


def portions_of(number_of, total, most, lean, full):
    portions = [(1 << 20) // math.isqrt(rank ** lean) + 1 for rank in range(1, number_of + 1)]
    largest = most if full else min(most, max(-(-total // number_of), total * portions[0] // sum(portions)))
    least = 1 if total - largest >= number_of - 1 else 0
    given, surplus = [largest] + [least] * (number_of - 1), total - largest - least * (number_of - 1)
    while surplus > 0:
        free = [i for i in range(1, number_of) if given[i] < largest] or [i for i in range(1, number_of) if given[i] < most]
        mass, budget = sum([portions[i] for i in free]), surplus
        for i in free:
            addition = min(most - given[i], max(1, budget * portions[i] // mass), surplus)
            given[i] = given[i] + addition
            surplus = surplus - addition
    return np.array(given)


def normal_values(rng, dims, spread, limit, cuts=(), held_as=jnp.bfloat16):
    values = spread * jax.random.normal(rng, dims, jnp.float32)
    if cuts:
        values = values * level_of(rng, dims, cuts, -0.22, 0.18)
    return jnp.clip(values, -limit, limit).astype(held_as)


def setup_inputs(seed: int = 0) -> dict:
    splits = jax.random.split(jax.random.key(seed), 10)
    hidden = normal_values(splits[0], (N_SECTION, ROWS, MODEL_WIDTH), 1.0, 6.0, ((0, 8), (2, 32)))
    attention_norm_scale = jnp.clip(1.0 + 0.18 * jax.random.normal(splits[1], (MODEL_WIDTH,), jnp.float32), 0.1, 1.9)
    joined_projection_weight = normal_values(splits[2], (N_SECTION, MODEL_WIDTH, JOINED_COLUMNS), MODEL_WIDTH ** -0.5, 0.0625, ((0, 8), (2, 32)))
    adapter_down_weight = normal_values(splits[3], (N_SECTION, ADAPTER_COUNT, MODEL_WIDTH, ADAPTER_RANK), MODEL_WIDTH ** -0.5, 0.0625, ((0, 8), (1, 32)))
    adapter_up_weight = normal_values(splits[4], (N_SECTION, ADAPTER_COUNT, ADAPTER_RANK, JOINED_COLUMNS), ADAPTER_RANK ** -0.5, 0.75, ((0, 8), (1, 32)))
    cached_key_rows = draw_cached_key_rows(jax.random.fold_in(splits[9], 71), 0)
    cached_value_rows = normal_values(splits[6], (N_SECTION, ROWS, CTX, KVD), 1.0, 6.0, ((0, 8), (2, 32)))
    row_adapter_index_keys = jax.random.split(jax.random.fold_in(splits[7], 1), N_SECTION * ROWS // ROWS)
    row_adapter_index_turns = jax.random.permutation(jax.random.fold_in(splits[7], 3), N_SECTION * ROWS // ROWS)
    row_adapter_index = jax.vmap(lambda own, number: assign_block(jax.random.fold_in(splits[7], 2), own, number, ROWS, ADAPTER_COUNT, 1, MOST, 2))(row_adapter_index_keys, row_adapter_index_turns).reshape((N_SECTION, ROWS, 1))
    lengths = jax.vmap(lambda own: ragged_sizes(own, ROWS, ROWS * CTX // 2, CTX - 1, 2))(jax.random.split(splits[8], N_SECTION)).reshape((N_SECTION, ROWS)).astype(jnp.int32)
    return dict(hidden=hidden, attention_norm_scale=attention_norm_scale, joined_projection_weight=joined_projection_weight, adapter_down_weight=adapter_down_weight, adapter_up_weight=adapter_up_weight, cached_key_rows=cached_key_rows, cached_value_rows=cached_value_rows, row_adapter_index=row_adapter_index, lengths=lengths)


EPS = 1e-05
ADAPTER_SCALE = 0.5
NEGATIVE = -1e+30

def normalize(rows, attention_norm_scale):
    wide = rows.astype(jnp.float32)
    inverse = lax.rsqrt(lax.optimization_barrier(jnp.mean(wide * wide, axis=-1, keepdims=True)) + EPS)
    return (wide * inverse * attention_norm_scale.astype(jnp.float32)).astype(jnp.bfloat16)

def relay_section_attention(hidden_rows, attention_norm_scale, weight, down_all, up_all, keys_all, values_all, chosen, used):
    normed = normalize(hidden_rows, attention_norm_scale)
    base = jnp.dot(normed, weight, preferred_element_type=jnp.float32)
    down_rows = down_all[chosen].astype(jnp.float32)
    reduced_rows = jnp.einsum('rd,rdk->rk', normed.astype(jnp.float32), down_rows)
    reduced_rows = lax.optimization_barrier(reduced_rows.astype(jnp.bfloat16)).astype(jnp.float32)
    up_weight_rows = up_all[chosen].astype(jnp.float32)
    adapter_update = jnp.einsum('tg,tgz->tz', reduced_rows, up_weight_rows) * ADAPTER_SCALE
    joined = lax.optimization_barrier((base + adapter_update).astype(jnp.bfloat16)).astype(jnp.float32)
    groups = H // KVH
    queries = joined[:, :QD].reshape(ROWS, KVH, groups, HD)
    fresh_keys = joined[:, QD:QD + KVD].reshape(ROWS, KVH, HD)
    fresh_values = joined[:, QD + KVD:].reshape(ROWS, KVH, HD)
    keys = keys_all.astype(jnp.float32).reshape(ROWS, CTX, KVH, HD)
    values = values_all.astype(jnp.float32).reshape(ROWS, CTX, KVH, HD)
    factor = 1.0 / math.sqrt(HD)
    scores = jnp.einsum('rkgd,rpkd->rkgp', queries, keys) * factor
    valid = (jnp.arange(CTX, dtype=jnp.int32)[None, :] < used[:, None])[:, None, None, :]
    scores = jnp.where(valid, scores, NEGATIVE)
    own_score = jnp.einsum('rkgd,rkd->rkg', queries, fresh_keys) * factor
    top = jnp.maximum(lax.optimization_barrier(jnp.max(scores, axis=-1)), own_score)
    weights = jnp.where(valid, jnp.exp(scores - top[..., None]), 0.0)
    own_weight = jnp.exp(own_score - top)
    total = lax.optimization_barrier(jnp.sum(weights, axis=-1)) + own_weight
    rounded = lax.optimization_barrier(weights.astype(jnp.bfloat16)).astype(jnp.float32)
    own_rounded = lax.optimization_barrier(own_weight.astype(jnp.bfloat16)).astype(jnp.float32)
    mixed = jnp.einsum('rkgp,rpkd->rkgd', rounded, values)
    mixed = mixed + own_rounded[..., None] * fresh_values[:, :, None, :]
    return (mixed / total[..., None]).reshape(ROWS, QD).astype(jnp.bfloat16)

def reference(hidden, attention_norm_scale, joined_projection_weight, adapter_down_weight, adapter_up_weight, cached_key_rows, cached_value_rows, row_adapter_index, lengths):
    context_outputs = []
    for relay_section_index in range(N_SECTION):
        context_outputs.append(relay_section_attention(hidden[relay_section_index], attention_norm_scale, joined_projection_weight[relay_section_index], adapter_down_weight[relay_section_index], adapter_up_weight[relay_section_index], cached_key_rows[relay_section_index], cached_value_rows[relay_section_index], row_adapter_index[relay_section_index, :, 0], lengths[relay_section_index]))
    stacked = jnp.stack(context_outputs, axis=0)
    return (jnp.roll(hidden, 1, axis=0), jnp.roll(stacked, 1, axis=0))
```

```python
import math

import jax
import jax.numpy as jnp
from jax import lax
from jax.experimental import pallas as pl
from jax.experimental.pallas import tpu as pltpu
from jax.sharding import PartitionSpec as P

H = 64
KVH = 8
HD = 128
MOST = 2
ROWS = 24
TP = 32
SPAN = 32
QUAD = 4
HEADS_HERE = H // TP
OWN = ROWS * HEADS_HERE
SLOT = 64
PART = 56

EPS = 1e-05
ADAPTER_SCALE = 0.5
NEGATIVE = -1e30
FLOOR = -1e20
FACTOR = 1.0 / math.sqrt(HD)


def passed_along(array, axis, by):
    devices = lax.axis_size(axis)
    return lax.ppermute(array, axis, [(i, (i + by) % devices) for i in range(devices)])


def to_all(piece, width):
    copies = jnp.broadcast_to(piece[None], (width,) + piece.shape)
    return lax.all_to_all(copies, "tp", 0, 0)


def on_vmem(kernel, mebibytes, out_shape, scratch, *arguments):
    vmem = pl.BlockSpec(memory_space=pltpu.VMEM)
    return pl.pallas_call(
        kernel,
        out_shape=out_shape,
        in_specs=[vmem if a.dtype != jnp.int32 else pl.BlockSpec(memory_space=pltpu.SMEM) for a in arguments],
        out_specs=jax.tree.map(lambda _: vmem, out_shape),
        scratch_shapes=scratch,
        compiler_params=pltpu.CompilerParams(vmem_limit_bytes=mebibytes * 1024 * 1024),
    )(*arguments)


def low_lanes(shape):
    return lax.broadcasted_iota(jnp.int32, shape, len(shape) - 1) < HD // 2


def pack_kernel(device_ref, base_ref, spread_ref, received_ref, slots_ref):
    received = received_ref[...].reshape(TP * 8, HD)
    tiles = []
    for k in range(3):
        change = jnp.dot(spread_ref[k], received, preferred_element_type=jnp.float32)
        tiles.append(base_ref[:, k * HD : (k + 1) * HD] + change)
    odd = device_ref[0] % 2 == 1
    turned = [pltpu.roll(tile, HD // 2, 1) for tile in tiles]
    low = low_lanes((ROWS, HD))
    first = jnp.where(odd, jnp.where(low, turned[0], turned[1]), tiles[0])
    second = jnp.where(odd, jnp.where(low, turned[1], turned[2]), tiles[1])
    part = jnp.where(odd, tiles[0], tiles[2])
    turned_part = jnp.where(odd, turned[0], turned[2])
    low = low_lanes((8, HD))
    even_pair = jnp.where(low, part[0:8], turned_part[8:16])
    odd_pair = jnp.where(low, part[8:16], turned_part[0:8])
    pair = jnp.where(odd, odd_pair, even_pair)
    last = jnp.where(odd, turned_part[16:24], part[16:24])
    slot = jnp.concatenate([first, second, pair, last], axis=0).astype(jnp.bfloat16)
    for t in range(TP):
        slots_ref[t] = slot


def attention_kernel(device_ref, slots_ref, keys_ref, values_ref, bias_ref, sent_ref, own_ref, own_value_ref, query, fresh, result, levels):
    low = low_lanes((8, HD))

    def put(head, rows):
        if head < H:
            query[head // 2, pl.ds(head % 2, ROWS, stride=2), :] = rows
        else:
            fresh[head - H, pl.ds(0, ROWS, stride=2), :] = rows
            fresh[head - H, pl.ds(1, ROWS, stride=2), :] = rows

    for p in range(TP // 2):
        even = slots_ref[2 * p].astype(jnp.float32)
        odd = slots_ref[2 * p + 1].astype(jnp.float32)
        put(5 * p, even[0:24])
        put(5 * p + 1, even[24:48])
        middle = jnp.where(low, odd[48:56], even[48:56])
        put(
            5 * p + 2,
            jnp.concatenate(
                [
                    jnp.where(low, even[48:56], odd[48:56]),
                    pltpu.roll(middle, HD // 2, 1),
                    jnp.where(low, even[56:64], odd[56:64]),
                ],
                axis=0,
            ),
        )
        put(5 * p + 3, odd[0:24])
        put(5 * p + 4, odd[24:48])

    device = device_ref[0]
    group = device // (TP // KVH)
    own_level = jnp.sum(query[device] * fresh[group], axis=1, keepdims=True) * FACTOR
    own_ref[...] = jnp.broadcast_to(own_level, (OWN, HD))
    own_value_ref[...] = fresh[KVH + group]

    quads = ROWS // QUAD
    rows = QUAD * SPAN
    lane = lax.broadcasted_iota(jnp.int32, (HD, HD), 1)
    for gg in range(2):
        for q in range(quads):
            left = jnp.concatenate([query[16 * gg + j, 8 * q : 8 * q + 8, :] for j in range(16)], axis=0)
            turned = jnp.transpose(left)
            parts = [jnp.where(lane // 32 == i, turned, 0.0).astype(jnp.bfloat16) for i in range(4)]
            right = jnp.concatenate(parts, axis=0)
            keys = keys_ref[QUAD * q : QUAD * (q + 1), :, 512 * gg : 512 * (gg + 1)].reshape(rows, 512)
            scores = jnp.dot(keys, right, preferred_element_type=jnp.float32) * FACTOR + bias_ref[q]
            top = jnp.maximum(jnp.max(scores, axis=0, keepdims=True), FLOOR)
            weights = jnp.exp(scores - top)
            total = jnp.sum(weights, axis=0, keepdims=True)
            some = total > 0.0
            safe = jnp.where(some, total, 1.0)
            levels[gg, q : q + 1, :] = jnp.where(some, top + jnp.log(safe), NEGATIVE)
            weights = jnp.transpose(weights * (1.0 / safe)).astype(jnp.bfloat16)
            for i in range(4):
                g = 4 * gg + i
                values = values_ref[QUAD * q : QUAD * (q + 1), :, g * HD : (g + 1) * HD].reshape(rows, HD)
                mixed = jnp.dot(weights[32 * i : 32 * i + 32], values, preferred_element_type=jnp.float32)
                for j in range(4):
                    result[4 * g + j, 8 * q : 8 * q + 8, :] = mixed[8 * j : 8 * j + 8]
    sub = lax.broadcasted_iota(jnp.int32, (8, HD), 0)
    diagonal = lax.broadcasted_iota(jnp.int32, (8, HD), 1) // 8 == sub
    for gg in range(2):
        slanted = pltpu.roll(levels[gg], 0, 1, stride=8, stride_axis=0)
        for j in range(16):
            line = pltpu.roll(slanted, (HD - 8 * j) % HD, 1) if j else slanted
            line = jnp.sum(jnp.where(diagonal & (sub < quads), line, 0.0), axis=0, keepdims=True)
            high = line.astype(jnp.bfloat16).astype(jnp.float32)
            middle = (line - high).astype(jnp.bfloat16).astype(jnp.float32)
            rest = line - high - middle
            lines = jnp.where(sub == 0, high, jnp.where(sub == 1, middle, jnp.where(sub == 2, rest, 0.0)))
            t = 16 * gg + j
            sent_ref[t] = jnp.concatenate([result[t], lines], axis=0).astype(jnp.bfloat16)


def combine_kernel(arrived_ref, own_ref, own_value_ref, context_ref):
    eye = lax.broadcasted_iota(jnp.int32, (OWN, HD), 0) == lax.broadcasted_iota(jnp.int32, (OWN, HD), 1)
    own_level = jnp.sum(jnp.where(eye, own_ref[...], 0.0), axis=0, keepdims=True)
    lines = []
    for t in range(TP):
        terms = arrived_ref[t].astype(jnp.float32)[OWN:PART]
        lines.append(jnp.sum(terms, axis=0, keepdims=True))
    levels = jnp.concatenate(lines, axis=0)
    highest = jnp.maximum(jnp.max(levels, axis=0, keepdims=True), own_level)
    shares = jnp.exp(levels - highest)
    own_share = jnp.exp(own_level - highest)
    whole = jnp.sum(shares, axis=0, keepdims=True) + own_share
    own_share = jnp.broadcast_to(own_share / whole, (8, HD))
    shares = jnp.concatenate([shares / whole, own_share], axis=0)
    columns = jnp.transpose(jnp.concatenate([shares, jnp.zeros((HD - TP - 8, HD), jnp.float32)], axis=0))
    total = columns[0:OWN, TP : TP + 1] * own_value_ref[...]
    for t in range(TP):
        total = total + columns[0:OWN, t : t + 1] * arrived_ref[t].astype(jnp.float32)[0:OWN]
    context_ref[...] = total


def on_device(
    hidden,
    attention_norm_scale,
    joined_projection_weight,
    adapter_down_weight,
    adapter_up_weight,
    cached_key_rows,
    cached_value_rows,
    row_adapter_index,
    lengths,
):
    width = lax.axis_size("tp")
    device = lax.axis_index("tp")
    where = device.astype(jnp.int32).reshape(1)
    rows_here = hidden[0]
    batch, features = rows_here.shape
    moved_rows = passed_along(rows_here, "section", 1)

    chosen = row_adapter_index[0, :, 0]
    same = chosen[:, None] == chosen[None, :]
    earlier = jnp.arange(batch)[None, :] < jnp.arange(batch)[:, None]
    place = jnp.sum(same & earlier, axis=1)
    slots = jnp.arange(MOST)
    mine = (chosen[None, :] == device) & (place[None, :] == slots[:, None])
    slot_of_row = chosen * 8 + place * 3
    lines = slot_of_row[None, :, None] + jnp.arange(3)[:, None, None]
    spread = (lines == jnp.arange(width * 8)[None, None, :]).astype(jnp.bfloat16)

    span = cached_key_rows.shape[2]
    used = lengths[0].reshape(batch // QUAD, QUAD, 1, 1, 1, 1)
    seen = device * span + jnp.arange(span, dtype=jnp.int32).reshape(span, 1, 1, 1) < used
    seen = seen & jnp.eye(QUAD, dtype=bool).reshape(1, QUAD, 1, 1, QUAD, 1)
    bias = jnp.where(seen, 0.0, NEGATIVE).astype(jnp.float32)
    bias = jnp.broadcast_to(bias, (batch // QUAD, QUAD, span, 16, QUAD, HEADS_HERE))
    bias = bias.reshape(batch // QUAD, QUAD * span, HD)

    pieces = to_all(rows_here, width)
    gathered = pieces.transpose(1, 0, 2).reshape(batch, width * features)
    wide = gathered.astype(jnp.float32)
    inverse = lax.rsqrt(jnp.mean(wide * wide, axis=-1, keepdims=True) + EPS)
    normed = (wide * inverse * attention_norm_scale).astype(jnp.bfloat16)
    reduced_rows = jnp.dot(normed, adapter_down_weight[0, 0], preferred_element_type=jnp.float32)
    picked = jnp.dot(
        mine.astype(jnp.bfloat16),
        reduced_rows.astype(jnp.bfloat16),
        preferred_element_type=jnp.float32,
    ).astype(jnp.bfloat16)
    update = jnp.dot(picked, adapter_up_weight[0, 0], preferred_element_type=jnp.float32)
    columns = update.shape[1] // width
    update = (update * ADAPTER_SCALE).astype(jnp.bfloat16).reshape(MOST, width, columns)
    update = jnp.pad(update.transpose(1, 0, 2), ((0, 0), (0, 0), (0, 3 * HD - columns)))
    update = jnp.pad(update.reshape(width, 3 * MOST, HD), ((0, 0), (0, 8 - 3 * MOST), (0, 0)))
    received = lax.all_to_all(update, "tp", 0, 0)
    base = jnp.dot(normed, joined_projection_weight[0], preferred_element_type=jnp.float32)
    base = jnp.pad(base, ((0, 0), (0, 3 * HD - columns)))
    slots = on_vmem(
        pack_kernel,
        4,
        jax.ShapeDtypeStruct((TP, SLOT, HD), jnp.bfloat16),
        [],
        where,
        base,
        spread,
        received,
    )
    joined = lax.all_to_all(slots, "tp", 0, 0)

    sent, own, own_value = on_vmem(
        attention_kernel,
        12,
        (
            jax.ShapeDtypeStruct((TP, PART, HD), jnp.bfloat16),
            jax.ShapeDtypeStruct((OWN, HD), jnp.float32),
            jax.ShapeDtypeStruct((OWN, HD), jnp.float32),
        ),
        [
            pltpu.VMEM((TP, OWN, HD), jnp.float32),
            pltpu.VMEM((2 * KVH, OWN, HD), jnp.float32),
            pltpu.VMEM((TP, OWN, HD), jnp.float32),
            pltpu.VMEM((2, 8, HD), jnp.float32),
        ],
        where,
        joined,
        cached_key_rows[0],
        cached_value_rows[0],
        bias,
    )
    arrived = lax.all_to_all(sent, "tp", 0, 0)
    context = on_vmem(
        combine_kernel, 4, jax.ShapeDtypeStruct((OWN, HD), jnp.float32), [], arrived, own, own_value
    )
    context = context.reshape(batch, HEADS_HERE * HD).astype(jnp.bfloat16)
    moved_context = passed_along(context, "section", 1)
    return (moved_rows[None], moved_context[None])


def solution(mesh):
    return jax.shard_map(
        on_device,
        mesh=mesh,
        in_specs=(
            P("section", None, "tp"),
            P(),
            P("section", None, "tp"),
            P("section", "tp", None, None),
            P("section", "tp", None, None),
            P("section", None, "tp", None),
            P("section", None, "tp", None),
            P("section", None, None),
            P("section", None),
        ),
        out_specs=(P("section", None, "tp"), P("section", None, "tp")),
        check_vma=False,
    )
```

```python
import math

import jax
import jax.numpy as jnp
from jax import lax
from jax.experimental import pallas as pl
from jax.experimental.pallas import tpu as pltpu
from jax.sharding import PartitionSpec as P

H = 64
KVH = 8
HD = 128
MOST = 2
ROWS = 24
TP = 32
SPAN = 32
QUAD = 4
HEADS_HERE = H // TP
OWN = ROWS * HEADS_HERE
SLOT = 64
PART = 56

EPS = 1e-05
ADAPTER_SCALE = 0.5
NEGATIVE = -1e30
FLOOR = -1e20
FACTOR = 1.0 / math.sqrt(HD)


def passed_along(array, axis, by):
    devices = lax.axis_size(axis)
    return lax.ppermute(array, axis, [(i, (i + by) % devices) for i in range(devices)])


def call(kernel, mebibytes, out_shape, scratch, *arguments):
    vmem, hbm = pl.BlockSpec(memory_space=pltpu.VMEM), pl.BlockSpec(memory_space=pltpu.HBM)
    far = [isinstance(a, Far) for a in arguments]
    values = [pltpu.with_memory_space_constraint(a.array, pltpu.HBM) if f else a for a, f in zip(arguments, far)]
    return pl.pallas_call(
        kernel,
        out_shape=out_shape,
        in_specs=[hbm if f else vmem for f in far],
        out_specs=tuple(hbm if getattr(o, "memory_space", None) == pltpu.HBM else vmem for o in out_shape),
        scratch_shapes=scratch,
        compiler_params=pltpu.CompilerParams(vmem_limit_bytes=mebibytes * 1024 * 1024),
    )(*values)


class Far:
    def __init__(self, array):
        self.array = array


def low_lanes(shape):
    return lax.broadcasted_iota(jnp.int32, shape, len(shape) - 1) < HD // 2


def pack_kernel(base_ref, spread_ref, received_ref, slots_ref):
    received = received_ref[...].reshape(TP * 8, HD)
    tiles = []
    for k in range(3):
        change = jnp.dot(spread_ref[k], received, preferred_element_type=jnp.float32)
        tiles.append(base_ref[:, k * HD : (k + 1) * HD] + change)
    odd = lax.axis_index("tp") % 2 == 1
    turned = [pltpu.roll(tile, HD // 2, 1) for tile in tiles]
    low = low_lanes((ROWS, HD))
    first = jnp.where(odd, jnp.where(low, turned[0], turned[1]), tiles[0])
    second = jnp.where(odd, jnp.where(low, turned[1], turned[2]), tiles[1])
    part = jnp.where(odd, tiles[0], tiles[2])
    turned_part = jnp.where(odd, turned[0], turned[2])
    low = low_lanes((8, HD))
    even_pair = jnp.where(low, part[0:8], turned_part[8:16])
    odd_pair = jnp.where(low, part[8:16], turned_part[0:8])
    pair = jnp.where(odd, odd_pair, even_pair)
    last = jnp.where(odd, turned_part[16:24], part[16:24])
    slot = jnp.concatenate([first, second, pair, last], axis=0).astype(jnp.bfloat16)
    for t in range(TP):
        slots_ref[t] = slot


def attention_kernel(
    slots_ref, used_ref, keys_far, values_far, moved_ref, sent_ref, own_ref, own_value_ref, kept_ref,
    query, fresh, result, levels, biases, keys_ref, values_ref, sent, load_sem, sent_sem, kept_sem,
):
    quads = ROWS // QUAD
    loads = []
    for i, (far, near) in enumerate(((keys_far, keys_ref), (values_far, values_ref))):
        loads.append([])
        for q in range(3):
            part = pl.ds(8 * q, 8)
            loads[i].append(pltpu.make_async_copy(far.at[part], near.at[part], load_sem.at[i, q]))
            loads[i][q].start()
    keep = pltpu.make_async_copy(moved_ref, kept_ref, kept_sem)
    keep.start()
    levels[...] = jnp.full(levels.shape, NEGATIVE, jnp.float32)
    row_lane = lax.broadcasted_iota(jnp.int32, (SPAN, HD), 1) // 2 % QUAD
    position = lax.axis_index("tp") * SPAN + lax.broadcasted_iota(jnp.int32, (SPAN, HD), 0)
    for row in range(ROWS):
        seen = (position < used_ref[row : row + 1, :]) & (row_lane == row % QUAD)
        at = SPAN * (row % QUAD)
        biases[row // QUAD, at : at + SPAN, :] = jnp.where(seen, 0.0, NEGATIVE)
    low = low_lanes((8, HD))

    def put(head, rows):
        if head < H:
            query[head // 2, pl.ds(head % 2, ROWS, stride=2), :] = rows
        else:
            fresh[head - H, pl.ds(0, ROWS, stride=2), :] = rows
            fresh[head - H, pl.ds(1, ROWS, stride=2), :] = rows

    for p in range(TP // 2):
        even = slots_ref[2 * p].astype(jnp.float32)
        odd = slots_ref[2 * p + 1].astype(jnp.float32)
        put(5 * p, even[0:24])
        put(5 * p + 1, even[24:48])
        middle = jnp.where(low, odd[48:56], even[48:56])
        put(
            5 * p + 2,
            jnp.concatenate(
                [
                    jnp.where(low, even[48:56], odd[48:56]),
                    pltpu.roll(middle, HD // 2, 1),
                    jnp.where(low, even[56:64], odd[56:64]),
                ],
                axis=0,
            ),
        )
        put(5 * p + 3, odd[0:24])
        put(5 * p + 4, odd[24:48])

    device = lax.axis_index("tp")
    group = device // (TP // KVH)
    own_level = jnp.sum(query[device] * fresh[group], axis=1, keepdims=True) * FACTOR
    own_ref[...] = jnp.broadcast_to(own_level, (OWN, HD))
    own_value_ref[...] = fresh[KVH + group]

    rows = QUAD * SPAN
    lane = lax.broadcasted_iota(jnp.int32, (HD, HD), 1)
    for load in loads[0]:
        load.wait()
    kept = {}
    for gg in range(2):
        for q in range(quads):
            left = jnp.concatenate([query[16 * gg + j, 8 * q : 8 * q + 8, :] for j in range(16)], axis=0)
            turned = jnp.transpose(left)
            parts = [jnp.where(lane // 32 == i, turned, 0.0).astype(jnp.bfloat16) for i in range(4)]
            right = jnp.concatenate(parts, axis=0)
            keys = keys_ref[QUAD * q : QUAD * (q + 1), :, 512 * gg : 512 * (gg + 1)].reshape(rows, 512)
            scores = jnp.dot(keys, right, preferred_element_type=jnp.float32) * FACTOR + biases[q]
            top = jnp.maximum(jnp.max(scores, axis=0, keepdims=True), FLOOR)
            weights = jnp.exp(scores - top)
            total = jnp.sum(weights, axis=0, keepdims=True)
            some = total > 0.0
            safe = jnp.where(some, total, 1.0)
            levels[gg, q : q + 1, :] = jnp.where(some, top + jnp.log(safe), NEGATIVE)
            kept[gg, q] = jnp.transpose(weights * (1.0 / safe)).astype(jnp.bfloat16)
    for load in loads[1]:
        load.wait()
    eighth = lax.broadcasted_iota(jnp.int32, (8, HD), 1) // 8
    stores = []
    for gg in range(2):
        level = levels[gg]
        high = level.astype(jnp.bfloat16).astype(jnp.float32)
        middle = (level - high).astype(jnp.bfloat16).astype(jnp.float32)
        rest = pltpu.roll(level - high - middle, 16, 1)
        middle = pltpu.roll(middle, 8, 1)
        for q in range(quads):
            for i in range(4):
                g = 4 * gg + i
                part = values_ref[QUAD * q : QUAD * (q + 1), :, g * HD : (g + 1) * HD].reshape(rows, HD)
                mixed = jnp.dot(kept[gg, q][32 * i : 32 * i + 32], part, preferred_element_type=jnp.float32)
                for j in range(4):
                    result[4 * g + j, 8 * q : 8 * q + 8, :] = mixed[8 * j : 8 * j + 8]
        for j in range(16):
            lines = jnp.where(eighth == j, high, jnp.where(eighth == (j + 1) % 16, middle, rest))
            t = 16 * gg + j
            sent[t] = jnp.concatenate([result[t], lines], axis=0).astype(jnp.bfloat16)
        half = pl.ds(16 * gg, 16)
        stores.append(pltpu.make_async_copy(sent.at[half], sent_ref.at[half], sent_sem.at[gg]))
        stores[-1].start()
    for store in stores:
        store.wait()
    keep.wait()


def eighth_lanes():
    return lax.broadcasted_iota(jnp.int32, (8, HD), 1) < 8


def combine_kernel(arrived_ref, own_ref, own_value_ref, context_ref):
    quads = ROWS // QUAD
    turn = (HD - 8 * (lax.axis_index("tp") % 16)) % HD
    eye = lax.broadcasted_iota(jnp.int32, (8, HD), 0) == lax.broadcasted_iota(jnp.int32, (8, HD), 1)
    own = [
        jnp.sum(jnp.where(eye, own_ref[8 * q : 8 * q + 8, :], 0.0), axis=0, keepdims=True) for q in range(quads)
    ]
    own = jnp.concatenate(own + [jnp.zeros((8 - quads, HD), jnp.float32)], axis=0)
    levels = []
    for t in range(TP):
        terms = arrived_ref[t].astype(jnp.float32)[OWN:PART]
        levels.append(terms + pltpu.roll(terms, HD - 8, 1) + pltpu.roll(terms, HD - 16, 1))
    levels = [jnp.where(eighth_lanes(), pltpu.roll(level, turn, 1), 0.0) for level in levels]
    highest = own
    for level in levels:
        highest = jnp.maximum(highest, level)
    shares = [jnp.exp(level - highest) for level in levels]
    own = jnp.exp(own - highest)
    whole = own
    for share in shares:
        whole = whole + share
    scale = 1.0 / whole
    shares = [share * scale for share in shares]
    columns = [jnp.transpose(jnp.concatenate(shares[16 * i : 16 * i + 16], axis=0)) for i in range(2)]
    own = jnp.transpose(jnp.concatenate([own * scale] + [jnp.zeros((HD - 8, HD), jnp.float32)], axis=0))
    totals = [own[0:8, q : q + 1] * own_value_ref[8 * q : 8 * q + 8, :] for q in range(quads)]
    for t in range(TP):
        rows = arrived_ref[t].astype(jnp.float32)
        for q in range(quads):
            at = 8 * (t % 16) + q
            totals[q] = totals[q] + columns[t // 16][0:8, at : at + 1] * rows[8 * q : 8 * q + 8]
    context_ref[...] = jnp.concatenate(totals, axis=0)


def on_device(
    hidden,
    attention_norm_scale,
    joined_projection_weight,
    adapter_down_weight,
    adapter_up_weight,
    cached_key_rows,
    cached_value_rows,
    row_adapter_index,
    lengths,
):
    width = lax.axis_size("tp")
    device = lax.axis_index("tp")
    rows_here = hidden[0]
    batch, features = rows_here.shape
    moved_rows = passed_along(rows_here, "section", 1)

    chosen = row_adapter_index[0, :, 0]
    same = chosen[:, None] == chosen[None, :]
    earlier = jnp.arange(batch)[None, :] < jnp.arange(batch)[:, None]
    place = jnp.sum(same & earlier, axis=1)
    mine = (chosen[None, :] == device) & (place[None, :] == jnp.arange(MOST)[:, None])
    slot_of_row = chosen * 8 + place * 3
    lines = slot_of_row[None, :, None] + jnp.arange(3)[:, None, None]
    spread = (lines == jnp.arange(width * 8)[None, None, :]).astype(jnp.bfloat16)

    cache = cached_key_rows.shape[1:]
    copies = jnp.broadcast_to(rows_here[None], (width, batch, features))
    pieces = lax.all_to_all(copies, "tp", 0, 0)
    gathered = pieces.transpose(1, 0, 2).reshape(batch, width * features)
    wide = gathered.astype(jnp.float32)
    inverse = lax.rsqrt(jnp.mean(wide * wide, axis=-1, keepdims=True) + EPS)
    normed = (wide * inverse * attention_norm_scale).astype(jnp.bfloat16)
    shrunk = jnp.dot(normed, adapter_down_weight[0, 0], preferred_element_type=jnp.float32)
    picked = jnp.dot(
        mine.astype(jnp.bfloat16), shrunk.astype(jnp.bfloat16), preferred_element_type=jnp.float32
    ).astype(jnp.bfloat16)
    update = jnp.dot(picked, adapter_up_weight[0, 0], preferred_element_type=jnp.float32)
    columns = update.shape[1] // width
    update = (update * ADAPTER_SCALE).astype(jnp.bfloat16).reshape(MOST, width, columns)
    update = jnp.pad(update.transpose(1, 0, 2), ((0, 0), (0, 0), (0, 3 * HD - columns)))
    update = jnp.pad(update.reshape(width, 3 * MOST, HD), ((0, 0), (0, 8 - 3 * MOST), (0, 0)))
    received = lax.all_to_all(update, "tp", 0, 0)
    base = jnp.dot(normed, joined_projection_weight[0], preferred_element_type=jnp.float32)
    base = jnp.pad(base, ((0, 0), (0, 3 * HD - base.shape[1])))
    (slots,) = call(
        pack_kernel,
        4,
        (jax.ShapeDtypeStruct((TP, SLOT, HD), jnp.bfloat16),),
        [],
        base,
        spread,
        received,
    )
    joined = lax.all_to_all(slots, "tp", 0, 0)

    sent, own, own_value, moved_rows = call(
        attention_kernel,
        12,
        (
            pltpu.HBM((TP, PART, HD), jnp.bfloat16),
            jax.ShapeDtypeStruct((OWN, HD), jnp.float32),
            jax.ShapeDtypeStruct((OWN, HD), jnp.float32),
            pltpu.HBM((batch, features), jnp.bfloat16),
        ),
        [
            pltpu.VMEM((TP, OWN, HD), jnp.float32),
            pltpu.VMEM((2 * KVH, OWN, HD), jnp.float32),
            pltpu.VMEM((TP, OWN, HD), jnp.float32),
            pltpu.VMEM((2, 8, HD), jnp.float32),
            pltpu.VMEM((batch // QUAD, QUAD * SPAN, HD), jnp.float32),
            pltpu.VMEM(cache, jnp.bfloat16),
            pltpu.VMEM(cache, jnp.bfloat16),
            pltpu.VMEM((TP, PART, HD), jnp.bfloat16),
            pltpu.SemaphoreType.DMA((2, 3)),
            pltpu.SemaphoreType.DMA((2,)),
            pltpu.SemaphoreType.DMA,
        ],
        joined,
        jnp.broadcast_to(lengths[0][:, None], (batch, HD)),
        Far(cached_key_rows[0]),
        Far(cached_value_rows[0]),
        moved_rows,
    )
    arrived = lax.all_to_all(sent, "tp", 0, 0)
    (context,) = call(
        combine_kernel,
        4,
        (jax.ShapeDtypeStruct((OWN, HD), jnp.float32),),
        [],
        arrived,
        own,
        own_value,
    )
    context = context.reshape(batch, HEADS_HERE * HD).astype(jnp.bfloat16)
    moved_context = passed_along(context, "section", 1)
    return (moved_rows[None], moved_context[None])


def solution(mesh):
    return jax.shard_map(
        on_device,
        mesh=mesh,
        in_specs=(
            P("section", None, "tp"),
            P(),
            P("section", None, "tp"),
            P("section", "tp", None, None),
            P("section", "tp", None, None),
            P("section", None, "tp", None),
            P("section", None, "tp", None),
            P("section", None, None),
            P("section", None),
        ),
        out_specs=(P("section", None, "tp"), P("section", None, "tp")),
        check_vma=False,
    )
```

```python
import math

import jax
import jax.numpy as jnp
from jax import lax
from jax.experimental import pallas as pl
from jax.experimental.pallas import tpu as pltpu
from jax.sharding import PartitionSpec as P

H = 64
KVH = 8
HD = 128
MOST = 2
ROWS = 24
TP = 32
SPAN = 32
QUAD = 4
NEAR = 8
SHARE = ROWS // 2
GIVEN = SHARE // 2
QUADS = SHARE // QUAD
HEADS_HERE = H // TP
LINES = SHARE * HEADS_HERE
SLOT = 32
PART = LINES + 8

EPS = 1e-05
ADAPTER_SCALE = 0.5
NEGATIVE = -1e30
FLOOR = -1e20
FACTOR = 1.0 / math.sqrt(HD)


def passed_along(array, axis, by):
    devices = lax.axis_size(axis)
    return lax.ppermute(array, axis, [(i, (i + by) % devices) for i in range(devices)])


def call(kernel, mebibytes, out_shape, scratch, *arguments):
    vmem, hbm = pl.BlockSpec(memory_space=pltpu.VMEM), pl.BlockSpec(memory_space=pltpu.HBM)
    far = [isinstance(a, Far) for a in arguments]
    values = [pltpu.with_memory_space_constraint(a.array, pltpu.HBM) if f else a for a, f in zip(arguments, far)]
    return pl.pallas_call(
        kernel,
        out_shape=out_shape,
        in_specs=[hbm if f else vmem for f in far],
        out_specs=tuple(hbm if getattr(o, "memory_space", None) == pltpu.HBM else vmem for o in out_shape),
        scratch_shapes=scratch,
        compiler_params=pltpu.CompilerParams(vmem_limit_bytes=mebibytes * 1024 * 1024),
    )(*values)


class Far:
    def __init__(self, array):
        self.array = array


def low_lanes(shape):
    return lax.broadcasted_iota(jnp.int32, shape, len(shape) - 1) < HD // 2


def pack_kernel(base_ref, spread_ref, received_ref, *rest):
    slots_ref = rest[-1]
    received = received_ref[...].reshape(TP * 8, HD)
    tiles = []
    for k in range(3):
        change = jnp.dot(spread_ref[k], received, preferred_element_type=jnp.float32)
        tiles.append(base_ref[:, k * HD : (k + 1) * HD] + change)
    odd = lax.axis_index("tp") % 2 == 1
    turned = [pltpu.roll(tile, HD // 2, 1) for tile in tiles]
    low = low_lanes((ROWS, HD))
    first = jnp.where(odd, jnp.where(low, turned[0], turned[1]), tiles[0])
    second = jnp.where(odd, jnp.where(low, turned[1], turned[2]), tiles[1])
    part = jnp.where(odd, tiles[0], tiles[2])
    turned_part = jnp.where(odd, turned[0], turned[2])
    low = low_lanes((8, HD))
    upper = lax.broadcasted_iota(jnp.int32, (8, HD), 0) < 4
    slots = []
    for side in range(2):
        main = slice(16 * side, 16 * side + 8)
        firsts, seconds, parts, turned_parts = (v[8:16] for v in (first, second, part, turned_part))
        if side == 0:
            seconds = pltpu.roll(seconds, 4, 0)
        else:
            firsts, parts, turned_parts = (pltpu.roll(v, 4, 0) for v in (firsts, parts, turned_parts))
        left = jnp.where(upper, firsts, seconds)
        even_half = jnp.where(low, part[main], turned_parts)
        odd_half = jnp.where(low, parts, turned_part[main])
        half = jnp.where(odd, odd_half, even_half)
        slots.append(jnp.concatenate([first[main], second[main], left, half], axis=0).astype(jnp.bfloat16))
    for t in range(TP):
        slots_ref[t] = slots[t // NEAR % 2]


def attention_kernel(
    slots_ref, limit_ref, keys_far, values_far, keys_a, keys_b, values_a, values_b, moved_ref, sent_ref, kept_ref,
    query, fresh, result, levels, added, biases, keys_ref, values_ref, sent, load_sem, given_sem, sent_sem, kept_sem,
):
    device = lax.axis_index("tp")
    side = device // NEAR % 2
    caches = ((keys_far, keys_a, keys_b, keys_ref), (values_far, values_a, values_b, values_ref))

    def own_load(i, q):
        start = SHARE * side + QUAD * lax.rem(q + side, QUADS)
        far, near = caches[i][0], caches[i][3]
        return pltpu.make_async_copy(far.at[pl.ds(start, QUAD)], near.at[q, 0], load_sem.at[i, q])

    def given_load(i, p, on_side):
        row = (2 * p + QUAD * on_side) % SHARE
        far, near = caches[i][1 + row // GIVEN], caches[i][3]
        return pltpu.make_async_copy(
            far.at[pl.ds(row % GIVEN, 2)], near.at[p // 2, 1, pl.ds(2 * (p % 2), 2)], given_sem.at[i, p]
        )

    for i in range(2):
        for q in range(QUADS):
            own_load(i, q).start()
        for on_side in range(2):

            @pl.when(side == on_side)
            def _():
                for p in range(2 * QUADS):
                    given_load(i, p, on_side).start()

    keep = pltpu.make_async_copy(moved_ref, kept_ref, kept_sem)
    keep.start()
    levels[...] = jnp.full(levels.shape, NEGATIVE, jnp.float32)
    added[...] = jnp.zeros(added.shape, jnp.float32)
    row_lane = lax.broadcasted_iota(jnp.int32, (SPAN, HD), 1) // 2 % QUAD
    position = lax.broadcasted_iota(jnp.int32, (SPAN, HD), 0)
    for block in range(2):
        for row in range(SHARE):
            at = block * SHARE + row
            seen = (position < limit_ref[at : at + 1, :]) & (row_lane == row % QUAD)
            to = SPAN * (QUAD * block + row % QUAD)
            biases[row // QUAD, to : to + SPAN, :] = jnp.where(seen, 0.0, NEGATIVE)
    low = low_lanes((8, HD))

    def put(head, main, left):
        def store(ref, at, side):
            ref[at, pl.ds(side, 8, stride=2), :] = main
            ref[at, pl.ds(16 + side, 4, stride=2), :] = left[0:4]

        if head < H:
            store(query, head // 2, head % 2)
        else:
            store(fresh, head - H, 0)
            store(fresh, head - H, 1)

    for p in range(TP // 2):
        even = slots_ref[2 * p].astype(jnp.float32)
        odd = slots_ref[2 * p + 1].astype(jnp.float32)
        for head, tile in ((5 * p, even), (5 * p + 3, odd)):
            put(head, tile[0:8], tile[16:24])
            put(head + 1, tile[8:16], pltpu.roll(tile[16:24], 4, 0))
        left = pltpu.roll(jnp.where(low, odd[24:32], even[24:32]), HD // 2, 1)
        put(5 * p + 2, jnp.where(low, even[24:32], odd[24:32]), left)

    eighth = lax.broadcasted_iota(jnp.int32, (8, HD), 1) // 8
    eye = lax.broadcasted_iota(jnp.int32, (8, HD), 0) == lax.broadcasted_iota(jnp.int32, (8, HD), 1)
    own_devices = (device, device + NEAR - 2 * NEAR * side)
    own_lines = jnp.full((8, HD), NEGATIVE, jnp.float32)
    for at in own_devices:
        own = query[at] * fresh[at // (TP // KVH)]
        level = jnp.sum(own, axis=1, keepdims=True) * FACTOR
        lines = [
            jnp.sum(jnp.where(eye, level[8 * q : 8 * q + 8], 0.0), axis=0, keepdims=True) for q in range(QUADS)
        ]
        lines = jnp.concatenate(lines + [jnp.zeros((8 - QUADS, HD), jnp.float32)], axis=0)
        own_lines = jnp.where(eighth == at % 16, pltpu.roll(lines, 8 * (at % 16), 1), own_lines)

    rows = 2 * QUAD * SPAN
    lane = lax.broadcasted_iota(jnp.int32, (HD, HD), 1)
    for q in range(QUADS):
        own_load(0, q).wait()
    for p in range(2 * QUADS):
        given_load(0, p, 0).wait()
    kept = {}
    for gg in range(2):
        own_here = jnp.where(device // 16 == gg, own_lines, NEGATIVE)
        for q in range(QUADS):
            left = jnp.concatenate([query[16 * gg + j, 8 * q : 8 * q + 8, :] for j in range(16)], axis=0)
            turned = jnp.transpose(left)
            parts = [jnp.where(lane // 32 == i, turned, 0.0).astype(jnp.bfloat16) for i in range(4)]
            right = jnp.concatenate(parts, axis=0)
            keys = keys_ref[q, :, :, :, 512 * gg : 512 * (gg + 1)].reshape(rows, 512)
            scores = jnp.dot(keys, right, preferred_element_type=jnp.float32) * FACTOR + biases[q]
            own = own_here[q : q + 1, :]
            top = jnp.maximum(jnp.maximum(jnp.max(scores, axis=0, keepdims=True), own), FLOOR)
            weights = jnp.exp(scores - top)
            own = jnp.exp(own - top)
            total = jnp.sum(weights, axis=0, keepdims=True) + own
            some = total > 0.0
            safe = jnp.where(some, total, 1.0)
            levels[gg, q : q + 1, :] = jnp.where(some, top + jnp.log(safe), NEGATIVE)
            scale = 1.0 / safe
            added[q : q + 1, :] = added[q : q + 1, :] + own * scale
            kept[gg, q] = jnp.transpose(weights * scale).astype(jnp.bfloat16)
    own_terms = []
    for at in own_devices:
        lines = pltpu.roll(added[...], lax.rem(HD - 8 * (at % 16), HD), 1)
        columns = jnp.transpose(jnp.concatenate([lines, jnp.zeros((HD - 8, HD), jnp.float32)], axis=0))
        value = fresh[KVH + at // (TP // KVH)]
        terms = [columns[0:8, q : q + 1] * value[8 * q : 8 * q + 8] for q in range(QUADS)]
        own_terms.append(jnp.concatenate(terms, axis=0))
    for q in range(QUADS):
        own_load(1, q).wait()
    for p in range(2 * QUADS):
        given_load(1, p, 0).wait()
    stores = []
    for gg in range(2):
        level = levels[gg]
        high = level.astype(jnp.bfloat16).astype(jnp.float32)
        middle = (level - high).astype(jnp.bfloat16).astype(jnp.float32)
        rest = pltpu.roll(level - high - middle, 16, 1)
        middle = pltpu.roll(middle, 8, 1)
        for q in range(QUADS):
            for i in range(4):
                g = 4 * gg + i
                part = values_ref[q, :, :, :, g * HD : (g + 1) * HD].reshape(rows, HD)
                mixed = jnp.dot(kept[gg, q][32 * i : 32 * i + 32], part, preferred_element_type=jnp.float32)
                for j in range(4):
                    result[4 * g + j, 8 * q : 8 * q + 8, :] = mixed[8 * j : 8 * j + 8]
        for j in range(16):
            lines = jnp.where(eighth == j, high, jnp.where(eighth == (j + 1) % 16, middle, rest))
            t = 16 * gg + j
            whole = result[t]
            for at, terms in zip(own_devices, own_terms):
                whole = whole + jnp.where(at == t, terms, 0.0)
            sent[t] = jnp.concatenate([whole, lines], axis=0).astype(jnp.bfloat16)
        half = pl.ds(16 * gg, 16)
        stores.append(pltpu.make_async_copy(sent.at[half], sent_ref.at[half], sent_sem.at[gg]))
        stores[-1].start()
    for store in stores:
        store.wait()
    keep.wait()


def combine_kernel(arrived_ref, context_ref):
    turn = lax.rem(HD - 8 * (lax.axis_index("tp") % 16), HD)
    eight = lax.broadcasted_iota(jnp.int32, (8, HD), 1) < 8
    pieces = []
    for side in range(2):
        sources = [t for t in range(TP) if t // NEAR % 2 == side]
        levels = []
        for t in sources:
            terms = pltpu.roll(arrived_ref[t].astype(jnp.float32)[LINES:PART], turn, 1)
            terms = terms + pltpu.roll(terms, HD - 8, 1) + pltpu.roll(terms, HD - 16, 1)
            levels.append(jnp.where(eight, terms, 0.0))
        highest = levels[0]
        for level in levels[1:]:
            highest = jnp.maximum(highest, level)
        shares = [jnp.exp(level - highest) for level in levels]
        whole = shares[0]
        for share in shares[1:]:
            whole = whole + share
        scale = 1.0 / whole
        columns = jnp.transpose(jnp.concatenate([share * scale for share in shares], axis=0))
        totals = [jnp.zeros((8, HD), jnp.float32)] * QUADS
        for i, t in enumerate(sources):
            rows = arrived_ref[t].astype(jnp.float32)
            for q in range(QUADS):
                at = 8 * i + q
                totals[q] = totals[q] + columns[0:8, at : at + 1] * rows[8 * q : 8 * q + 8]
        pieces += totals if side == 0 else [totals[2], totals[0], totals[1]]
    context_ref[...] = jnp.concatenate(pieces, axis=0)


def on_device(
    hidden,
    attention_norm_scale,
    joined_projection_weight,
    adapter_down_weight,
    adapter_up_weight,
    cached_key_rows,
    cached_value_rows,
    row_adapter_index,
    lengths,
):
    width = lax.axis_size("tp")
    device = lax.axis_index("tp")
    rows_here = hidden[0]
    batch, features = rows_here.shape
    moved_rows = passed_along(rows_here, "section", 1)

    chosen = row_adapter_index[0, :, 0]
    same = chosen[:, None] == chosen[None, :]
    earlier = jnp.arange(batch)[None, :] < jnp.arange(batch)[:, None]
    place = jnp.sum(same & earlier, axis=1)
    mine = (chosen[None, :] == device) & (place[None, :] == jnp.arange(MOST)[:, None])
    slot_of_row = chosen * 8 + place * 3
    lines = slot_of_row[None, :, None] + jnp.arange(3)[:, None, None]
    spread = (lines == jnp.arange(width * 8)[None, None, :]).astype(jnp.bfloat16)

    side = device // NEAR % 2
    wide = width // NEAR
    at = [(y, z) for y in range(wide) for z in range(NEAR)]
    meetings = ([(y * NEAR + z, (y ^ 1) * NEAR + z) for y, z in at], [(y * NEAR + z, (wide - 1 - y) * NEAR + z) for y, z in at])
    given = []
    for cached in (cached_key_rows[0], cached_value_rows[0]):
        for i, pairs in enumerate(meetings):
            part = lax.dynamic_slice_in_dim(cached, SHARE * (1 - side) + GIVEN * i, GIVEN, 0)
            given.append(lax.ppermute(part, "tp", pairs))
    span = cached_key_rows.shape[2]
    used = lengths[0]
    turned = jnp.concatenate([used[SHARE + QUAD :], used[SHARE : SHARE + QUAD]])
    used = jnp.where(side == 0, used[:SHARE], turned)
    row = (jnp.arange(SHARE) + QUAD * side) % SHARE
    y, z = device // NEAR, device % NEAR
    giver = jnp.where(row < GIVEN, y ^ 1, wide - 1 - y) * NEAR + z
    limits = jnp.concatenate([used - span * device, used - span * giver])
    limits = jnp.broadcast_to(limits[:, None], (2 * SHARE, HD))
    near_cache = (QUADS, 2, QUAD) + cached_key_rows.shape[2:]
    copies = jnp.broadcast_to(rows_here[None], (width, batch, features))
    pieces = lax.all_to_all(copies, "tp", 0, 0)
    gathered = pieces.transpose(1, 0, 2).reshape(batch, width * features)
    wide = gathered.astype(jnp.float32)
    inverse = lax.rsqrt(jnp.mean(wide * wide, axis=-1, keepdims=True) + EPS)
    normed = (wide * inverse * attention_norm_scale).astype(jnp.bfloat16)
    shrunk = jnp.dot(normed, adapter_down_weight[0, 0], preferred_element_type=jnp.float32)
    picked = jnp.dot(
        mine.astype(jnp.bfloat16), shrunk.astype(jnp.bfloat16), preferred_element_type=jnp.float32
    ).astype(jnp.bfloat16)
    update = jnp.dot(picked, adapter_up_weight[0, 0], preferred_element_type=jnp.float32)
    columns = update.shape[1] // width
    update = (update * ADAPTER_SCALE).astype(jnp.bfloat16).reshape(MOST, width, columns)
    update = jnp.pad(update.transpose(1, 0, 2), ((0, 0), (0, 0), (0, 3 * HD - columns)))
    update = jnp.pad(update.reshape(width, 3 * MOST, HD), ((0, 0), (0, 8 - 3 * MOST), (0, 0)))
    received = lax.all_to_all(update, "tp", 0, 0)
    base = jnp.dot(normed, joined_projection_weight[0], preferred_element_type=jnp.float32)
    base = jnp.pad(base, ((0, 0), (0, 3 * HD - base.shape[1])))
    (slots,) = call(
        pack_kernel,
        4,
        (jax.ShapeDtypeStruct((TP, SLOT, HD), jnp.bfloat16),),
        [],
        base,
        spread,
        received,
        *[Far(part) for part in given],
    )
    joined = lax.all_to_all(slots, "tp", 0, 0)

    sent, moved_rows = call(
        attention_kernel,
        12,
        (pltpu.HBM((TP, PART, HD), jnp.bfloat16), pltpu.HBM((batch, features), jnp.bfloat16)),
        [
            pltpu.VMEM((TP, LINES, HD), jnp.float32),
            pltpu.VMEM((2 * KVH, LINES, HD), jnp.float32),
            pltpu.VMEM((TP, LINES, HD), jnp.float32),
            pltpu.VMEM((2, 8, HD), jnp.float32),
            pltpu.VMEM((8, HD), jnp.float32),
            pltpu.VMEM((QUADS, 2 * QUAD * SPAN, HD), jnp.float32),
            pltpu.VMEM(near_cache, jnp.bfloat16),
            pltpu.VMEM(near_cache, jnp.bfloat16),
            pltpu.VMEM((TP, PART, HD), jnp.bfloat16),
            pltpu.SemaphoreType.DMA((2, QUADS)),
            pltpu.SemaphoreType.DMA((2, 2 * QUADS)),
            pltpu.SemaphoreType.DMA((2,)),
            pltpu.SemaphoreType.DMA,
        ],
        joined,
        limits,
        Far(cached_key_rows[0]),
        Far(cached_value_rows[0]),
        *[Far(part) for part in given],
        moved_rows,
    )
    arrived = lax.all_to_all(sent, "tp", 0, 0)
    (context,) = call(combine_kernel, 4, (jax.ShapeDtypeStruct((ROWS * HEADS_HERE, HD), jnp.float32),), [], arrived)
    context = context.reshape(batch, HEADS_HERE * HD).astype(jnp.bfloat16)
    moved_context = passed_along(context, "section", 1)
    return (moved_rows[None], moved_context[None])


def solution(mesh):
    return jax.shard_map(
        on_device,
        mesh=mesh,
        in_specs=(
            P("section", None, "tp"),
            P(),
            P("section", None, "tp"),
            P("section", "tp", None, None),
            P("section", "tp", None, None),
            P("section", None, "tp", None),
            P("section", None, "tp", None),
            P("section", None, None),
            P("section", None),
        ),
        out_specs=(P("section", None, "tp"), P("section", None, "tp")),
        check_vma=False,
    )
```

```python
import math

import jax
import jax.numpy as jnp
from jax import lax
from jax.experimental import pallas as pl
from jax.experimental.pallas import tpu as pltpu
from jax.sharding import PartitionSpec as P

H = 64
KVH = 8
HD = 128
MOST = 2
ROWS = 24
TP = 32
SPAN = 32
QUAD = 4
NEAR = 8
SHARE = ROWS // 2
GIVEN = SHARE // 2
QUADS = SHARE // QUAD
HEADS_HERE = H // TP
LINES = SHARE * HEADS_HERE
SLOT = 32
PART = LINES + 8

EPS = 1e-05
ADAPTER_SCALE = 0.5
NEGATIVE = -1e30
FLOOR = -1e20
FACTOR = 1.0 / math.sqrt(HD)


def passed_along(array, axis, by):
    devices = lax.axis_size(axis)
    return lax.ppermute(array, axis, [(i, (i + by) % devices) for i in range(devices)])


def call(kernel, mebibytes, out_shape, scratch, *arguments):
    vmem, hbm = pl.BlockSpec(memory_space=pltpu.VMEM), pl.BlockSpec(memory_space=pltpu.HBM)
    specs, values = [], []
    for a in arguments:
        far = isinstance(a, Far)
        specs.append(pl.BlockSpec(memory_space=a.space) if far else vmem)
        values.append(a.array if far else a)
        if far and a.space == pltpu.HBM:
            values[-1] = pltpu.with_memory_space_constraint(a.array, pltpu.HBM)
    return pl.pallas_call(
        kernel,
        out_shape=out_shape,
        in_specs=specs,
        out_specs=tuple(hbm if getattr(o, "memory_space", None) == pltpu.HBM else vmem for o in out_shape),
        scratch_shapes=scratch,
        compiler_params=pltpu.CompilerParams(vmem_limit_bytes=mebibytes * 1024 * 1024),
    )(*values)


class Far:
    def __init__(self, array, space=pltpu.HBM):
        self.array, self.space = array, space


def low_lanes(shape):
    return lax.broadcasted_iota(jnp.int32, shape, len(shape) - 1) < HD // 2


def pack_kernel(base_ref, spread_ref, received_ref, *rest):
    slots_ref = rest[-1]
    received = received_ref[...].reshape(TP * 8, HD)
    tiles = []
    for k in range(3):
        change = jnp.dot(spread_ref[k], received, preferred_element_type=jnp.float32)
        tiles.append(base_ref[:, k * HD : (k + 1) * HD] + change)
    odd = lax.axis_index("tp") % 2 == 1
    turned = [pltpu.roll(tile, HD // 2, 1) for tile in tiles]
    low = low_lanes((ROWS, HD))
    first = jnp.where(odd, jnp.where(low, turned[0], turned[1]), tiles[0])
    second = jnp.where(odd, jnp.where(low, turned[1], turned[2]), tiles[1])
    part = jnp.where(odd, tiles[0], tiles[2])
    turned_part = jnp.where(odd, turned[0], turned[2])
    low = low_lanes((8, HD))
    upper = lax.broadcasted_iota(jnp.int32, (8, HD), 0) < 4
    slots = []
    for side in range(2):
        main = slice(16 * side, 16 * side + 8)
        firsts, seconds, parts, turned_parts = (v[8:16] for v in (first, second, part, turned_part))
        if side == 0:
            seconds = pltpu.roll(seconds, 4, 0)
        else:
            firsts, parts, turned_parts = (pltpu.roll(v, 4, 0) for v in (firsts, parts, turned_parts))
        left = jnp.where(upper, firsts, seconds)
        even_half = jnp.where(low, part[main], turned_parts)
        odd_half = jnp.where(low, parts, turned_part[main])
        half = jnp.where(odd, odd_half, even_half)
        slots.append(jnp.concatenate([first[main], second[main], left, half], axis=0).astype(jnp.bfloat16))
    for t in range(TP):
        slots_ref[t] = slots[t // NEAR % 2]


def attention_kernel(
    slots_ref, used_ref, keys_own, values_far, keys_a, keys_b, values_a, values_b, moved_ref, sent_ref, kept_ref,
    query, fresh, result, levels, added, biases, values_own, given_va, given_vb, load_sem, kept_sem,
):
    device = lax.axis_index("tp")
    side = device // NEAR % 2
    first_giver = device + NEAR - 2 * NEAR * side
    second_giver = (TP // NEAR - 1 - device // NEAR) * NEAR + device % NEAR
    loads = [
        pltpu.make_async_copy(values_far.at[pl.ds(SHARE * side, SHARE)], values_own, load_sem.at[0]),
        pltpu.make_async_copy(values_a, given_va, load_sem.at[1]),
        pltpu.make_async_copy(values_b, given_vb, load_sem.at[2]),
    ]
    for load in loads:
        load.start()

    def lined_up(own, given_a, given_b, q, lanes):
        parts = [own[QUAD * q : QUAD * (q + 1), :, lanes]]
        for row in range(QUAD * q, QUAD * (q + 1), 2):
            given, at = (given_a, row) if row < GIVEN else (given_b, row - GIVEN)
            parts.append(given[at : at + 2, :, lanes])
        return jnp.concatenate([part.reshape(-1, part.shape[-1]) for part in parts], axis=0)

    keep = pltpu.make_async_copy(moved_ref, kept_ref, kept_sem)
    keep.start()
    levels[...] = jnp.full(levels.shape, NEGATIVE, jnp.float32)
    added[...] = jnp.zeros(added.shape, jnp.float32)
    row_lane = lax.broadcasted_iota(jnp.int32, (SPAN, HD), 1) // 2 % QUAD
    position = lax.broadcasted_iota(jnp.int32, (SPAN, HD), 0)
    for block in range(2):
        for row in range(SHARE):
            start = (device, first_giver if row < GIVEN else second_giver)[block] * SPAN
            seen = (position < used_ref[SHARE * side + row] - start) & (row_lane == row % QUAD)
            to = SPAN * (QUAD * block + row % QUAD)
            biases[row // QUAD, to : to + SPAN, :] = jnp.where(seen, 0.0, NEGATIVE)
    low = low_lanes((8, HD))

    def put(head, main, left):
        def store(ref, at, which):
            ref[at, pl.ds(8 * side + which, 8, stride=2), :] = main
            ref[at, pl.ds(16 - 16 * side + which, 4, stride=2), :] = left[0:4]

        if head < H:
            store(query, head // 2, head % 2)
        else:
            store(fresh, head - H, 0)
            store(fresh, head - H, 1)

    for p in range(TP // 2):
        even = slots_ref[2 * p].astype(jnp.float32)
        odd = slots_ref[2 * p + 1].astype(jnp.float32)
        for head, tile in ((5 * p, even), (5 * p + 3, odd)):
            put(head, tile[0:8], tile[16:24])
            put(head + 1, tile[8:16], pltpu.roll(tile[16:24], 4, 0))
        left = pltpu.roll(jnp.where(low, odd[24:32], even[24:32]), HD // 2, 1)
        put(5 * p + 2, jnp.where(low, even[24:32], odd[24:32]), left)

    eighth = lax.broadcasted_iota(jnp.int32, (8, HD), 1) // 8
    eye = lax.broadcasted_iota(jnp.int32, (8, HD), 0) == lax.broadcasted_iota(jnp.int32, (8, HD), 1)
    own_devices = (device, first_giver)
    own_lines = jnp.full((8, HD), NEGATIVE, jnp.float32)
    for at in own_devices:
        own = query[at] * fresh[at // (TP // KVH)]
        level = jnp.sum(own, axis=1, keepdims=True) * FACTOR
        lines = [
            jnp.sum(jnp.where(eye, level[8 * q : 8 * q + 8], 0.0), axis=0, keepdims=True) for q in range(QUADS)
        ]
        lines = jnp.concatenate(lines + [jnp.zeros((8 - QUADS, HD), jnp.float32)], axis=0)
        own_lines = jnp.where(eighth == at % 16, pltpu.roll(lines, 8 * (at % 16), 1), own_lines)

    lane = lax.broadcasted_iota(jnp.int32, (HD, HD), 1)
    kept = {}
    for gg in range(2):
        own_here = jnp.where(device // 16 == gg, own_lines, NEGATIVE)
        for q in range(QUADS):
            left = jnp.concatenate([query[16 * gg + j, 8 * q : 8 * q + 8, :] for j in range(16)], axis=0)
            turned = jnp.transpose(left)
            parts = [jnp.where(lane // 32 == i, turned, 0.0).astype(jnp.bfloat16) for i in range(4)]
            right = jnp.concatenate(parts, axis=0)
            keys = lined_up(keys_own, keys_a, keys_b, q, slice(512 * gg, 512 * (gg + 1)))
            scores = jnp.dot(keys, right, preferred_element_type=jnp.float32) * FACTOR + biases[q]
            own = own_here[q : q + 1, :]
            top = jnp.maximum(jnp.maximum(jnp.max(scores, axis=0, keepdims=True), own), FLOOR)
            weights = jnp.exp(scores - top)
            own = jnp.exp(own - top)
            total = jnp.sum(weights, axis=0, keepdims=True) + own
            some = total > 0.0
            safe = jnp.where(some, total, 1.0)
            levels[gg, q : q + 1, :] = jnp.where(some, top + jnp.log(safe), NEGATIVE)
            scale = 1.0 / safe
            added[q : q + 1, :] = added[q : q + 1, :] + own * scale
            kept[gg, q] = jnp.transpose(weights * scale).astype(jnp.bfloat16)
    own_terms = []
    for at in own_devices:
        lines = pltpu.roll(added[...], lax.rem(HD - 8 * (at % 16), HD), 1)
        columns = jnp.transpose(jnp.concatenate([lines, jnp.zeros((HD - 8, HD), jnp.float32)], axis=0))
        value = fresh[KVH + at // (TP // KVH)]
        terms = [columns[0:8, q : q + 1] * value[8 * q : 8 * q + 8] for q in range(QUADS)]
        own_terms.append(jnp.concatenate(terms, axis=0))
    for load in loads:
        load.wait()
    for gg in range(2):
        level = levels[gg]
        high = level.astype(jnp.bfloat16).astype(jnp.float32)
        middle = (level - high).astype(jnp.bfloat16).astype(jnp.float32)
        rest = pltpu.roll(level - high - middle, 16, 1)
        middle = pltpu.roll(middle, 8, 1)
        for q in range(QUADS):
            for i in range(4):
                g = 4 * gg + i
                part = lined_up(values_own, given_va, given_vb, q, slice(g * HD, (g + 1) * HD))
                mixed = jnp.dot(kept[gg, q][32 * i : 32 * i + 32], part, preferred_element_type=jnp.float32)
                for j in range(4):
                    result[4 * g + j, 8 * q : 8 * q + 8, :] = mixed[8 * j : 8 * j + 8]
        for j in range(16):
            lines = jnp.where(eighth == j, high, jnp.where(eighth == (j + 1) % 16, middle, rest))
            t = 16 * gg + j
            whole = result[t]
            for at, terms in zip(own_devices, own_terms):
                whole = whole + jnp.where(at == t, terms, 0.0)
            sent_ref[t] = jnp.concatenate([whole, lines], axis=0).astype(jnp.bfloat16)
    keep.wait()


def combine_kernel(arrived_ref, context_ref):
    turn = lax.rem(HD - 8 * (lax.axis_index("tp") % 16), HD)
    eight = lax.broadcasted_iota(jnp.int32, (8, HD), 1) < 8
    pieces = []
    for side in range(2):
        sources = [t for t in range(TP) if t // NEAR % 2 == side]
        levels = []
        for t in sources:
            terms = pltpu.roll(arrived_ref[t].astype(jnp.float32)[LINES:PART], turn, 1)
            terms = terms + pltpu.roll(terms, HD - 8, 1) + pltpu.roll(terms, HD - 16, 1)
            levels.append(jnp.where(eight, terms, 0.0))
        highest = levels[0]
        for level in levels[1:]:
            highest = jnp.maximum(highest, level)
        shares = [jnp.exp(level - highest) for level in levels]
        whole = shares[0]
        for share in shares[1:]:
            whole = whole + share
        scale = 1.0 / whole
        columns = jnp.transpose(jnp.concatenate([share * scale for share in shares], axis=0))
        totals = [jnp.zeros((8, HD), jnp.float32)] * QUADS
        for i, t in enumerate(sources):
            rows = arrived_ref[t].astype(jnp.float32)
            for q in range(QUADS):
                at = 8 * i + q
                totals[q] = totals[q] + columns[0:8, at : at + 1] * rows[8 * q : 8 * q + 8]
        pieces += totals
    context_ref[...] = jnp.concatenate(pieces, axis=0)


def on_device(
    hidden,
    attention_norm_scale,
    joined_projection_weight,
    adapter_down_weight,
    adapter_up_weight,
    cached_key_rows,
    cached_value_rows,
    row_adapter_index,
    lengths,
):
    width = lax.axis_size("tp")
    device = lax.axis_index("tp")
    rows_here = hidden[0]
    batch, features = rows_here.shape
    moved_rows = passed_along(rows_here, "section", 1)

    chosen = row_adapter_index[0, :, 0]
    same = chosen[:, None] == chosen[None, :]
    earlier = jnp.arange(batch)[None, :] < jnp.arange(batch)[:, None]
    place = jnp.sum(same & earlier, axis=1)
    mine = (chosen[None, :] == device) & (place[None, :] == jnp.arange(MOST)[:, None])
    slot_of_row = chosen * 8 + place * 3
    lines = slot_of_row[None, :, None] + jnp.arange(3)[:, None, None]
    spread = (lines == jnp.arange(width * 8)[None, None, :]).astype(jnp.bfloat16)

    side = device // NEAR % 2
    wide = width // NEAR
    at = [(y, z) for y in range(wide) for z in range(NEAR)]
    meetings = ([(y * NEAR + z, (y ^ 1) * NEAR + z) for y, z in at], [(y * NEAR + z, (wide - 1 - y) * NEAR + z) for y, z in at])
    given = []
    for cached in (cached_key_rows[0], cached_value_rows[0]):
        for i, pairs in enumerate(meetings):
            part = lax.dynamic_slice_in_dim(cached, SHARE * (1 - side) + GIVEN * i, GIVEN, 0)
            given.append(lax.ppermute(part, "tp", pairs))
    span = cached_key_rows.shape[2]
    own_keys = lax.dynamic_slice_in_dim(cached_key_rows[0], SHARE * side, SHARE, 0)
    copies = jnp.broadcast_to(rows_here[None], (width, batch, features))
    pieces = lax.all_to_all(copies, "tp", 0, 0)
    gathered = pieces.transpose(1, 0, 2).reshape(batch, width * features)
    wide = gathered.astype(jnp.float32)
    inverse = lax.rsqrt(jnp.mean(wide * wide, axis=-1, keepdims=True) + EPS)
    normed = (wide * inverse * attention_norm_scale).astype(jnp.bfloat16)
    shrunk = jnp.dot(normed, adapter_down_weight[0, 0], preferred_element_type=jnp.float32)
    picked = jnp.dot(
        mine.astype(jnp.bfloat16), shrunk.astype(jnp.bfloat16), preferred_element_type=jnp.float32
    ).astype(jnp.bfloat16)
    update = jnp.dot(picked, adapter_up_weight[0, 0], preferred_element_type=jnp.float32)
    columns = update.shape[1] // width
    update = (update * ADAPTER_SCALE).astype(jnp.bfloat16).reshape(MOST, width, columns)
    update = jnp.pad(update.transpose(1, 0, 2), ((0, 0), (0, 0), (0, 3 * HD - columns)))
    update = jnp.pad(update.reshape(width, 3 * MOST, HD), ((0, 0), (0, 8 - 3 * MOST), (0, 0)))
    received = lax.all_to_all(update, "tp", 0, 0)
    base = jnp.dot(normed, joined_projection_weight[0], preferred_element_type=jnp.float32)
    base = jnp.pad(base, ((0, 0), (0, 3 * HD - base.shape[1])))
    (slots,) = call(
        pack_kernel,
        4,
        (jax.ShapeDtypeStruct((TP, SLOT, HD), jnp.bfloat16),),
        [],
        base,
        spread,
        received,
        *[Far(part, pl.ANY) for part in (*given[:2], own_keys, moved_rows)],
        *[Far(part) for part in given[2:]],
    )
    joined = lax.all_to_all(slots, "tp", 0, 0)

    sent, moved_rows = call(
        attention_kernel,
        12,
        (jax.ShapeDtypeStruct((TP, PART, HD), jnp.bfloat16), pltpu.HBM((batch, features), jnp.bfloat16)),
        [
            pltpu.VMEM((TP, LINES, HD), jnp.float32),
            pltpu.VMEM((2 * KVH, LINES, HD), jnp.float32),
            pltpu.VMEM((TP, LINES, HD), jnp.float32),
            pltpu.VMEM((2, 8, HD), jnp.float32),
            pltpu.VMEM((8, HD), jnp.float32),
            pltpu.VMEM((QUADS, 2 * QUAD * SPAN, HD), jnp.float32),
            pltpu.VMEM((SHARE, span, KVH * HD), jnp.bfloat16),
            pltpu.VMEM((GIVEN, span, KVH * HD), jnp.bfloat16),
            pltpu.VMEM((GIVEN, span, KVH * HD), jnp.bfloat16),
            pltpu.SemaphoreType.DMA((3,)),
            pltpu.SemaphoreType.DMA,
        ],
        joined,
        Far(lengths[0], pltpu.SMEM),
        own_keys,
        Far(cached_value_rows[0]),
        *given[:2],
        *[Far(part) for part in given[2:]],
        moved_rows,
    )
    arrived = lax.all_to_all(sent, "tp", 0, 0)
    (context,) = call(combine_kernel, 4, (jax.ShapeDtypeStruct((ROWS * HEADS_HERE, HD), jnp.float32),), [], arrived)
    context = context.reshape(batch, HEADS_HERE * HD).astype(jnp.bfloat16)
    moved_context = passed_along(context, "section", 1)
    return (moved_rows[None], moved_context[None])


def solution(mesh):
    return jax.shard_map(
        on_device,
        mesh=mesh,
        in_specs=(
            P("section", None, "tp"),
            P(),
            P("section", None, "tp"),
            P("section", "tp", None, None),
            P("section", "tp", None, None),
            P("section", None, "tp", None),
            P("section", None, "tp", None),
            P("section", None, None),
            P("section", None),
        ),
        out_specs=(P("section", None, "tp"), P("section", None, "tp")),
        check_vma=False,
    )
```

```python
import math

import jax
import jax.numpy as jnp
from jax import lax
from jax.experimental import pallas as pl
from jax.experimental.pallas import tpu as pltpu
from jax.sharding import PartitionSpec as P

H = 64
KVH = 8
HD = 128
MOST = 2
ROWS = 24
TP = 32
SPAN = 32
QUAD = 4
NEAR = 8
SHARE = ROWS // 2
GIVEN = SHARE // 2
QUADS = SHARE // QUAD
HEADS_HERE = H // TP
LINES = SHARE * HEADS_HERE
SLOT = 32
PART = LINES + 8

EPS = 1e-05
ADAPTER_SCALE = 0.5
NEGATIVE = -1e30
FLOOR = -1e20
FACTOR = 1.0 / math.sqrt(HD)


def passed_along(array, axis, by):
    devices = lax.axis_size(axis)
    return lax.ppermute(array, axis, [(i, (i + by) % devices) for i in range(devices)])


def call(kernel, mebibytes, out_shape, scratch, *arguments):
    vmem, hbm = pl.BlockSpec(memory_space=pltpu.VMEM), pl.BlockSpec(memory_space=pltpu.HBM)
    specs, values = [], []
    for a in arguments:
        far = isinstance(a, Far)
        specs.append(pl.BlockSpec(memory_space=a.space) if far else vmem)
        values.append(a.array if far else a)
        if far and a.space == pltpu.HBM:
            values[-1] = pltpu.with_memory_space_constraint(a.array, pltpu.HBM)
    return pl.pallas_call(
        kernel,
        out_shape=out_shape,
        in_specs=specs,
        out_specs=tuple(hbm if getattr(o, "memory_space", None) == pltpu.HBM else vmem for o in out_shape),
        scratch_shapes=scratch,
        compiler_params=pltpu.CompilerParams(vmem_limit_bytes=mebibytes * 1024 * 1024),
    )(*values)


class Far:
    def __init__(self, array, space=pltpu.HBM):
        self.array, self.space = array, space


def low_lanes(shape):
    return lax.broadcasted_iota(jnp.int32, shape, len(shape) - 1) < HD // 2


def pack_kernel(base_ref, spread_ref, received_ref, *rest):
    slots_ref = rest[-1]
    received = received_ref[...].reshape(TP * 8, HD)
    tiles = []
    for k in range(3):
        change = jnp.dot(spread_ref[k], received, preferred_element_type=jnp.float32)
        tiles.append(base_ref[:, k * HD : (k + 1) * HD] + change)
    odd = lax.axis_index("tp") % 2 == 1
    turned = [pltpu.roll(tile, HD // 2, 1) for tile in tiles]
    low = low_lanes((ROWS, HD))
    first = jnp.where(odd, jnp.where(low, turned[0], turned[1]), tiles[0])
    second = jnp.where(odd, jnp.where(low, turned[1], turned[2]), tiles[1])
    part = jnp.where(odd, tiles[0], tiles[2])
    turned_part = jnp.where(odd, turned[0], turned[2])
    low = low_lanes((8, HD))
    upper = lax.broadcasted_iota(jnp.int32, (8, HD), 0) < 4
    slots = []
    for side in range(2):
        main = slice(16 * side, 16 * side + 8)
        firsts, seconds, parts, turned_parts = (v[8:16] for v in (first, second, part, turned_part))
        if side == 0:
            seconds = pltpu.roll(seconds, 4, 0)
        else:
            firsts, parts, turned_parts = (pltpu.roll(v, 4, 0) for v in (firsts, parts, turned_parts))
        left = jnp.where(upper, firsts, seconds)
        even_half = jnp.where(low, part[main], turned_parts)
        odd_half = jnp.where(low, parts, turned_part[main])
        half = jnp.where(odd, odd_half, even_half)
        slots.append(jnp.concatenate([first[main], second[main], left, half], axis=0).astype(jnp.bfloat16))
    for t in range(TP):
        slots_ref[t] = slots[t // NEAR % 2]


def attention_kernel(
    slots_ref, used_ref, keys_own, values_far, keys_a, keys_b, values_a, values_b, moved_ref, sent_ref, kept_ref,
    query, fresh, result, levels, added, biases, values_own, given_va, given_vb, load_sem, kept_sem,
):
    device = lax.axis_index("tp")
    side = device // NEAR % 2
    first_giver = device + NEAR - 2 * NEAR * side
    second_giver = (TP // NEAR - 1 - device // NEAR) * NEAR + device % NEAR
    loads = [
        pltpu.make_async_copy(values_far.at[pl.ds(SHARE * side, SHARE)], values_own, load_sem.at[0]),
        pltpu.make_async_copy(values_a, given_va, load_sem.at[1]),
        pltpu.make_async_copy(values_b, given_vb, load_sem.at[2]),
    ]
    for load in loads:
        load.start()

    def lined_up(own, given_a, given_b, q, lanes):
        parts = [own[QUAD * q : QUAD * (q + 1), :, lanes]]
        for row in range(QUAD * q, QUAD * (q + 1), 2):
            given, at = (given_a, row) if row < GIVEN else (given_b, row - GIVEN)
            parts.append(given[at : at + 2, :, lanes])
        return jnp.concatenate([part.reshape(-1, part.shape[-1]) for part in parts], axis=0)

    keep = pltpu.make_async_copy(moved_ref, kept_ref, kept_sem)
    keep.start()
    levels[...] = jnp.full(levels.shape, NEGATIVE, jnp.float32)
    added[...] = jnp.zeros(added.shape, jnp.float32)
    row_lane = lax.broadcasted_iota(jnp.int32, (SPAN, HD), 1) // 2 % QUAD
    position = lax.broadcasted_iota(jnp.int32, (SPAN, HD), 0)
    for block in range(2):
        for row in range(SHARE):
            start = (device, first_giver if row < GIVEN else second_giver)[block] * SPAN
            used = jnp.where(side == 0, used_ref[:, row : row + 1], used_ref[:, SHARE + row : SHARE + row + 1])
            seen = (position < used - start) & (row_lane == row % QUAD)
            to = SPAN * (QUAD * block + row % QUAD)
            biases[row // QUAD, to : to + SPAN, :] = jnp.where(seen, 0.0, NEGATIVE)
    low = low_lanes((8, HD))

    def put(head, main, left):
        def store(ref, at, which):
            ref[at, pl.ds(8 * side + which, 8, stride=2), :] = main
            ref[at, pl.ds(16 - 16 * side + which, 4, stride=2), :] = left[0:4]

        if head < H:
            store(query, head // 2, head % 2)
        else:
            store(fresh, head - H, 0)
            store(fresh, head - H, 1)

    for p in range(TP // 2):
        even = slots_ref[2 * p].astype(jnp.float32)
        odd = slots_ref[2 * p + 1].astype(jnp.float32)
        for head, tile in ((5 * p, even), (5 * p + 3, odd)):
            put(head, tile[0:8], tile[16:24])
            put(head + 1, tile[8:16], pltpu.roll(tile[16:24], 4, 0))
        left = pltpu.roll(jnp.where(low, odd[24:32], even[24:32]), HD // 2, 1)
        put(5 * p + 2, jnp.where(low, even[24:32], odd[24:32]), left)

    eighth = lax.broadcasted_iota(jnp.int32, (8, HD), 1) // 8
    eye = lax.broadcasted_iota(jnp.int32, (8, HD), 0) == lax.broadcasted_iota(jnp.int32, (8, HD), 1)
    own_devices = (device, first_giver)
    own_lines = jnp.full((8, HD), NEGATIVE, jnp.float32)
    for at in own_devices:
        own = query[at] * fresh[at // (TP // KVH)]
        level = jnp.sum(own, axis=1, keepdims=True) * FACTOR
        lines = [
            jnp.sum(jnp.where(eye, level[8 * q : 8 * q + 8], 0.0), axis=0, keepdims=True) for q in range(QUADS)
        ]
        lines = jnp.concatenate(lines + [jnp.zeros((8 - QUADS, HD), jnp.float32)], axis=0)
        own_lines = jnp.where(eighth == at % 16, pltpu.roll(lines, 8 * (at % 16), 1), own_lines)

    lane = lax.broadcasted_iota(jnp.int32, (HD, HD), 1)
    kept = {}
    for gg in range(2):
        own_here = jnp.where(device // 16 == gg, own_lines, NEGATIVE)
        for q in range(QUADS):
            left = jnp.concatenate([query[16 * gg + j, 8 * q : 8 * q + 8, :] for j in range(16)], axis=0)
            turned = jnp.transpose(left)
            parts = [jnp.where(lane // 32 == i, turned, 0.0).astype(jnp.bfloat16) for i in range(4)]
            right = jnp.concatenate(parts, axis=0)
            keys = lined_up(keys_own, keys_a, keys_b, q, slice(512 * gg, 512 * (gg + 1)))
            scores = jnp.dot(keys, right, preferred_element_type=jnp.float32) * FACTOR + biases[q]
            own = own_here[q : q + 1, :]
            top = jnp.maximum(jnp.maximum(jnp.max(scores, axis=0, keepdims=True), own), FLOOR)
            weights = jnp.exp(scores - top)
            own = jnp.exp(own - top)
            total = jnp.sum(weights, axis=0, keepdims=True) + own
            some = total > 0.0
            safe = jnp.where(some, total, 1.0)
            levels[gg, q : q + 1, :] = jnp.where(some, top + jnp.log(safe), NEGATIVE)
            scale = 1.0 / safe
            added[q : q + 1, :] = added[q : q + 1, :] + own * scale
            kept[gg, q] = jnp.transpose(weights * scale).astype(jnp.bfloat16)
    own_terms = []
    for at in own_devices:
        lines = pltpu.roll(added[...], lax.rem(HD - 8 * (at % 16), HD), 1)
        columns = jnp.transpose(jnp.concatenate([lines, jnp.zeros((HD - 8, HD), jnp.float32)], axis=0))
        value = fresh[KVH + at // (TP // KVH)]
        terms = [columns[0:8, q : q + 1] * value[8 * q : 8 * q + 8] for q in range(QUADS)]
        own_terms.append(jnp.concatenate(terms, axis=0))
    for load in loads:
        load.wait()
    for gg in range(2):
        level = levels[gg]
        high = level.astype(jnp.bfloat16).astype(jnp.float32)
        middle = (level - high).astype(jnp.bfloat16).astype(jnp.float32)
        rest = pltpu.roll(level - high - middle, 16, 1)
        middle = pltpu.roll(middle, 8, 1)
        for q in range(QUADS):
            for i in range(4):
                g = 4 * gg + i
                part = lined_up(values_own, given_va, given_vb, q, slice(g * HD, (g + 1) * HD))
                mixed = jnp.dot(kept[gg, q][32 * i : 32 * i + 32], part, preferred_element_type=jnp.float32)
                for j in range(4):
                    result[4 * g + j, 8 * q : 8 * q + 8, :] = mixed[8 * j : 8 * j + 8]
        for j in range(16):
            lines = jnp.where(eighth == j, high, jnp.where(eighth == (j + 1) % 16, middle, rest))
            t = 16 * gg + j
            whole = result[t]
            for at, terms in zip(own_devices, own_terms):
                whole = whole + jnp.where(at == t, terms, 0.0)
            sent_ref[t] = jnp.concatenate([whole, lines], axis=0).astype(jnp.bfloat16)
    keep.wait()


def combine_kernel(arrived_ref, context_ref):
    turn = lax.rem(HD - 8 * (lax.axis_index("tp") % 16), HD)
    eight = lax.broadcasted_iota(jnp.int32, (8, HD), 1) < 8
    pieces = []
    for side in range(2):
        sources = [t for t in range(TP) if t // NEAR % 2 == side]
        levels = []
        for t in sources:
            terms = pltpu.roll(arrived_ref[t].astype(jnp.float32)[LINES:PART], turn, 1)
            terms = terms + pltpu.roll(terms, HD - 8, 1) + pltpu.roll(terms, HD - 16, 1)
            levels.append(jnp.where(eight, terms, 0.0))
        highest = levels[0]
        for level in levels[1:]:
            highest = jnp.maximum(highest, level)
        shares = [jnp.exp(level - highest) for level in levels]
        whole = shares[0]
        for share in shares[1:]:
            whole = whole + share
        scale = 1.0 / whole
        columns = jnp.transpose(jnp.concatenate([share * scale for share in shares], axis=0))
        totals = [jnp.zeros((8, HD), jnp.float32)] * QUADS
        for i, t in enumerate(sources):
            rows = arrived_ref[t].astype(jnp.float32)
            for q in range(QUADS):
                at = 8 * i + q
                totals[q] = totals[q] + columns[0:8, at : at + 1] * rows[8 * q : 8 * q + 8]
        pieces += totals
    context_ref[...] = jnp.concatenate(pieces, axis=0)


def on_device(
    hidden,
    attention_norm_scale,
    joined_projection_weight,
    adapter_down_weight,
    adapter_up_weight,
    cached_key_rows,
    cached_value_rows,
    row_adapter_index,
    lengths,
):
    width = lax.axis_size("tp")
    device = lax.axis_index("tp")
    rows_here = hidden[0]
    batch, features = rows_here.shape
    moved_rows = passed_along(rows_here, "section", 1)

    chosen = row_adapter_index[0, :, 0]
    same = chosen[:, None] == chosen[None, :]
    earlier = jnp.arange(batch)[None, :] < jnp.arange(batch)[:, None]
    place = jnp.sum(same & earlier, axis=1)
    mine = (chosen[None, :] == device) & (place[None, :] == jnp.arange(MOST)[:, None])
    slot_of_row = chosen * 8 + place * 3
    lines = slot_of_row[None, :, None] + jnp.arange(3)[:, None, None]
    spread = (lines == jnp.arange(width * 8)[None, None, :]).astype(jnp.bfloat16)

    side = device // NEAR % 2
    wide = width // NEAR
    at = [(y, z) for y in range(wide) for z in range(NEAR)]
    meetings = ([(y * NEAR + z, (y ^ 1) * NEAR + z) for y, z in at], [(y * NEAR + z, (wide - 1 - y) * NEAR + z) for y, z in at])
    given = []
    for cached in (cached_key_rows[0], cached_value_rows[0]):
        for i, pairs in enumerate(meetings):
            part = lax.dynamic_slice_in_dim(cached, SHARE * (1 - side) + GIVEN * i, GIVEN, 0)
            given.append(lax.ppermute(part, "tp", pairs))
    span = cached_key_rows.shape[2]
    own_keys = lax.dynamic_slice_in_dim(cached_key_rows[0], SHARE * side, SHARE, 0)
    copies = jnp.broadcast_to(rows_here[None], (width, batch, features))
    pieces = lax.all_to_all(copies, "tp", 0, 0)
    gathered = pieces.transpose(1, 0, 2).reshape(batch, width * features)
    wide = gathered.astype(jnp.float32)
    inverse = lax.rsqrt(jnp.mean(wide * wide, axis=-1, keepdims=True) + EPS)
    normed = (wide * inverse * attention_norm_scale).astype(jnp.bfloat16)
    shrunk = jnp.dot(normed, adapter_down_weight[0, 0], preferred_element_type=jnp.float32)
    picked = jnp.dot(
        mine.astype(jnp.bfloat16), shrunk.astype(jnp.bfloat16), preferred_element_type=jnp.float32
    ).astype(jnp.bfloat16)
    update = jnp.dot(picked, adapter_up_weight[0, 0], preferred_element_type=jnp.float32)
    columns = update.shape[1] // width
    update = (update * ADAPTER_SCALE).astype(jnp.bfloat16).reshape(MOST, width, columns)
    update = jnp.pad(update.transpose(1, 0, 2), ((0, 0), (0, 0), (0, 3 * HD - columns)))
    update = jnp.pad(update.reshape(width, 3 * MOST, HD), ((0, 0), (0, 8 - 3 * MOST), (0, 0)))
    received = lax.all_to_all(update, "tp", 0, 0)
    base = jnp.dot(normed, joined_projection_weight[0], preferred_element_type=jnp.float32)
    base = jnp.pad(base, ((0, 0), (0, 3 * HD - base.shape[1])))
    (slots,) = call(
        pack_kernel,
        4,
        (jax.ShapeDtypeStruct((TP, SLOT, HD), jnp.bfloat16),),
        [],
        base,
        spread,
        received,
        *[Far(part, pl.ANY) for part in (*given[:2], own_keys, moved_rows)],
        *[Far(part) for part in given[2:]],
    )
    joined = lax.all_to_all(slots, "tp", 0, 0)

    sent, moved_rows = call(
        attention_kernel,
        12,
        (jax.ShapeDtypeStruct((TP, PART, HD), jnp.bfloat16), pltpu.HBM((batch, features), jnp.bfloat16)),
        [
            pltpu.VMEM((TP, LINES, HD), jnp.float32),
            pltpu.VMEM((2 * KVH, LINES, HD), jnp.float32),
            pltpu.VMEM((TP, LINES, HD), jnp.float32),
            pltpu.VMEM((2, 8, HD), jnp.float32),
            pltpu.VMEM((8, HD), jnp.float32),
            pltpu.VMEM((QUADS, 2 * QUAD * SPAN, HD), jnp.float32),
            pltpu.VMEM((SHARE, span, KVH * HD), jnp.bfloat16),
            pltpu.VMEM((GIVEN, span, KVH * HD), jnp.bfloat16),
            pltpu.VMEM((GIVEN, span, KVH * HD), jnp.bfloat16),
            pltpu.SemaphoreType.DMA((3,)),
            pltpu.SemaphoreType.DMA,
        ],
        joined,
        lengths,
        own_keys,
        Far(cached_value_rows[0]),
        *given[:2],
        *[Far(part) for part in given[2:]],
        moved_rows,
    )
    arrived = lax.all_to_all(sent, "tp", 0, 0)
    (context,) = call(combine_kernel, 4, (jax.ShapeDtypeStruct((ROWS * HEADS_HERE, HD), jnp.float32),), [], arrived)
    context = context.reshape(batch, HEADS_HERE * HD).astype(jnp.bfloat16)
    moved_context = passed_along(context, "section", 1)
    return (moved_rows[None], moved_context[None])


def solution(mesh):
    return jax.shard_map(
        on_device,
        mesh=mesh,
        in_specs=(
            P("section", None, "tp"),
            P(),
            P("section", None, "tp"),
            P("section", "tp", None, None),
            P("section", "tp", None, None),
            P("section", None, "tp", None),
            P("section", None, "tp", None),
            P("section", None, None),
            P("section", None),
        ),
        out_specs=(P("section", None, "tp"), P("section", None, "tp")),
        check_vma=False,
    )
```

```python
import math

import jax
import jax.numpy as jnp
from jax import lax
from jax.experimental import pallas as pl
from jax.experimental.pallas import tpu as pltpu
from jax.sharding import PartitionSpec as P

H = 64
KVH = 8
HD = 128
MOST = 2
ROWS = 24
TP = 32
SPAN = 32
QUAD = 4
NEAR = 8
SHARE = ROWS // 2
GIVEN = SHARE // 2
QUADS = SHARE // QUAD
HEADS_HERE = H // TP
LINES = SHARE * HEADS_HERE
SLOT = 32
PART = LINES + 8

EPS = 1e-05
ADAPTER_SCALE = 0.5
NEGATIVE = -1e30
FLOOR = -1e20
FACTOR = 1.0 / math.sqrt(HD)


def passed_along(array, axis, by):
    devices = lax.axis_size(axis)
    return lax.ppermute(array, axis, [(i, (i + by) % devices) for i in range(devices)])


def call(kernel, mebibytes, out_shape, scratch, *arguments):
    vmem, hbm = pl.BlockSpec(memory_space=pltpu.VMEM), pl.BlockSpec(memory_space=pltpu.HBM)
    specs, values = [], []
    for a in arguments:
        far = isinstance(a, Far)
        specs.append(pl.BlockSpec(memory_space=a.space) if far else vmem)
        values.append(a.array if far else a)
        if far and a.space == pltpu.HBM:
            values[-1] = pltpu.with_memory_space_constraint(a.array, pltpu.HBM)
    return pl.pallas_call(
        kernel,
        out_shape=out_shape,
        in_specs=specs,
        out_specs=tuple(hbm if getattr(o, "memory_space", None) == pltpu.HBM else vmem for o in out_shape),
        scratch_shapes=scratch,
        compiler_params=pltpu.CompilerParams(vmem_limit_bytes=mebibytes * 1024 * 1024),
    )(*values)


class Far:
    def __init__(self, array, space=pltpu.HBM):
        self.array, self.space = array, space


def low_lanes(shape):
    return lax.broadcasted_iota(jnp.int32, shape, len(shape) - 1) < HD // 2


def pack_kernel(base_ref, spread_ref, received_ref, *rest):
    slots_ref = rest[-1]
    received = received_ref[...].reshape(TP * 8, HD)
    tiles = []
    for k in range(3):
        change = jnp.dot(spread_ref[k], received, preferred_element_type=jnp.float32)
        tiles.append(base_ref[:, k * HD : (k + 1) * HD] + change)
    odd = lax.axis_index("tp") % 2 == 1
    turned = [pltpu.roll(tile, HD // 2, 1) for tile in tiles]
    low = low_lanes((ROWS, HD))
    first = jnp.where(odd, jnp.where(low, turned[0], turned[1]), tiles[0])
    second = jnp.where(odd, jnp.where(low, turned[1], turned[2]), tiles[1])
    part = jnp.where(odd, tiles[0], tiles[2])
    turned_part = jnp.where(odd, turned[0], turned[2])
    low = low_lanes((8, HD))
    upper = lax.broadcasted_iota(jnp.int32, (8, HD), 0) < 4
    slots = []
    for side in range(2):
        main = slice(16 * side, 16 * side + 8)
        firsts, seconds, parts, turned_parts = (v[8:16] for v in (first, second, part, turned_part))
        if side == 0:
            seconds = pltpu.roll(seconds, 4, 0)
        else:
            firsts, parts, turned_parts = (pltpu.roll(v, 4, 0) for v in (firsts, parts, turned_parts))
        left = jnp.where(upper, firsts, seconds)
        even_half = jnp.where(low, part[main], turned_parts)
        odd_half = jnp.where(low, parts, turned_part[main])
        half = jnp.where(odd, odd_half, even_half)
        slots.append(jnp.concatenate([first[main], second[main], left, half], axis=0).astype(jnp.bfloat16))
    for t in range(TP):
        slots_ref[t] = slots[t // NEAR % 2]


def attention_kernel(
    slots_ref, used_ref, keys_own, values_far, keys_a, keys_b, values_a, values_b, moved_ref, sent_ref, kept_ref,
    query, fresh, result, levels, added, biases, values_own, given_va, given_vb, load_sem, kept_sem,
):
    device = lax.axis_index("tp")
    side = device // NEAR % 2
    first_giver = device + NEAR - 2 * NEAR * side
    second_giver = (TP // NEAR - 1 - device // NEAR) * NEAR + device % NEAR
    loads = [
        pltpu.make_async_copy(values_far.at[pl.ds(SHARE * side, SHARE)], values_own, load_sem.at[0]),
        pltpu.make_async_copy(values_a, given_va, load_sem.at[1]),
        pltpu.make_async_copy(values_b, given_vb, load_sem.at[2]),
    ]
    for load in loads:
        load.start()

    def lined_up(own, given_a, given_b, q, lanes):
        parts = [own[QUAD * q : QUAD * (q + 1), :, lanes]]
        for row in range(QUAD * q, QUAD * (q + 1), 2):
            given, at = (given_a, row) if row < GIVEN else (given_b, row - GIVEN)
            parts.append(given[at : at + 2, :, lanes])
        return jnp.concatenate([part.reshape(-1, part.shape[-1]) for part in parts], axis=0)

    keep = pltpu.make_async_copy(moved_ref, kept_ref, kept_sem)
    keep.start()
    levels[...] = jnp.full(levels.shape, NEGATIVE, jnp.float32)
    added[...] = jnp.zeros(added.shape, jnp.float32)
    row_lane = lax.broadcasted_iota(jnp.int32, (SPAN, HD), 1) // 2 % QUAD
    position = lax.broadcasted_iota(jnp.int32, (SPAN, HD), 0)
    for block in range(2):
        for row in range(SHARE):
            start = (device, first_giver if row < GIVEN else second_giver)[block] * SPAN
            used = jnp.where(side == 0, used_ref[:, row : row + 1], used_ref[:, SHARE + row : SHARE + row + 1])
            seen = (position < used - start) & (row_lane == row % QUAD)
            to = SPAN * (QUAD * block + row % QUAD)
            biases[row // QUAD, to : to + SPAN, :] = jnp.where(seen, 0.0, NEGATIVE)
    low = low_lanes((8, HD))

    def put(head, main, left):
        def store(ref, at, which):
            ref[at, pl.ds(8 * side + which, 8, stride=2), :] = main
            ref[at, pl.ds(16 - 16 * side + which, 4, stride=2), :] = left[0:4]

        if head < H:
            store(query, head // 2, head % 2)
        else:
            store(fresh, head - H, 0)
            store(fresh, head - H, 1)

    for p in range(TP // 2):
        even = slots_ref[2 * p].astype(jnp.float32)
        odd = slots_ref[2 * p + 1].astype(jnp.float32)
        for head, tile in ((5 * p, even), (5 * p + 3, odd)):
            put(head, tile[0:8], tile[16:24])
            put(head + 1, tile[8:16], pltpu.roll(tile[16:24], 4, 0))
        left = pltpu.roll(jnp.where(low, odd[24:32], even[24:32]), HD // 2, 1)
        put(5 * p + 2, jnp.where(low, even[24:32], odd[24:32]), left)

    eighth = lax.broadcasted_iota(jnp.int32, (8, HD), 1) // 8
    eye = lax.broadcasted_iota(jnp.int32, (8, HD), 0) == lax.broadcasted_iota(jnp.int32, (8, HD), 1)
    own_devices = (device, first_giver)
    own_lines = jnp.full((8, HD), NEGATIVE, jnp.float32)
    for at in own_devices:
        own = query[at] * fresh[at // (TP // KVH)]
        level = jnp.sum(own, axis=1, keepdims=True) * FACTOR
        lines = [
            jnp.sum(jnp.where(eye, level[8 * q : 8 * q + 8], 0.0), axis=0, keepdims=True) for q in range(QUADS)
        ]
        lines = jnp.concatenate(lines + [jnp.zeros((8 - QUADS, HD), jnp.float32)], axis=0)
        own_lines = jnp.where(eighth == at % 16, pltpu.roll(lines, 8 * (at % 16), 1), own_lines)

    lane = lax.broadcasted_iota(jnp.int32, (HD, HD), 1)
    kept = {}
    for gg in range(2):
        own_here = jnp.where(device // 16 == gg, own_lines, NEGATIVE)
        for q in range(QUADS):
            left = jnp.concatenate([query[16 * gg + j, 8 * q : 8 * q + 8, :] for j in range(16)], axis=0)
            turned = jnp.transpose(left)
            parts = [jnp.where(lane // 32 == i, turned, 0.0).astype(jnp.bfloat16) for i in range(4)]
            right = jnp.concatenate(parts, axis=0)
            keys = lined_up(keys_own, keys_a, keys_b, q, slice(512 * gg, 512 * (gg + 1)))
            scores = jnp.dot(keys, right, preferred_element_type=jnp.float32) * FACTOR + biases[q]
            own = own_here[q : q + 1, :]
            top = jnp.maximum(jnp.maximum(jnp.max(scores, axis=0, keepdims=True), own), FLOOR)
            weights = jnp.exp(scores - top)
            own = jnp.exp(own - top)
            total = jnp.sum(weights, axis=0, keepdims=True) + own
            some = total > 0.0
            safe = jnp.where(some, total, 1.0)
            levels[gg, q : q + 1, :] = jnp.where(some, top + jnp.log(safe), NEGATIVE)
            scale = 1.0 / safe
            added[q : q + 1, :] = added[q : q + 1, :] + own * scale
            kept[gg, q] = jnp.transpose(weights * scale).astype(jnp.bfloat16)
    own_terms = []
    for at in own_devices:
        lines = pltpu.roll(added[...], lax.rem(HD - 8 * (at % 16), HD), 1)
        columns = jnp.transpose(jnp.concatenate([lines, jnp.zeros((HD - 8, HD), jnp.float32)], axis=0))
        value = fresh[KVH + at // (TP // KVH)]
        terms = [columns[0:8, q : q + 1] * value[8 * q : 8 * q + 8] for q in range(QUADS)]
        own_terms.append(jnp.concatenate(terms, axis=0))
    for gg in range(2):
        level = levels[gg]
        high = level.astype(jnp.bfloat16).astype(jnp.float32)
        middle = (level - high).astype(jnp.bfloat16).astype(jnp.float32)
        rest = pltpu.roll(level - high - middle, 16, 1)
        middle = pltpu.roll(middle, 8, 1)
        for j in range(16):
            lines = jnp.where(eighth == j, high, jnp.where(eighth == (j + 1) % 16, middle, rest))
            result[16 * gg + j, LINES:PART, :] = lines
    for load in loads:
        load.wait()
    for gg in range(2):
        for q in range(QUADS):
            for i in range(4):
                g = 4 * gg + i
                part = lined_up(values_own, given_va, given_vb, q, slice(g * HD, (g + 1) * HD))
                mixed = jnp.dot(kept[gg, q][32 * i : 32 * i + 32], part, preferred_element_type=jnp.float32)
                for j in range(4):
                    result[4 * g + j, 8 * q : 8 * q + 8, :] = mixed[8 * j : 8 * j + 8]
        for j in range(16):
            t = 16 * gg + j
            whole = result[t, 0:LINES]
            for at, terms in zip(own_devices, own_terms):
                whole = whole + jnp.where(at == t, terms, 0.0)
            sent_ref[t] = jnp.concatenate([whole, result[t, LINES:PART]], axis=0).astype(jnp.bfloat16)
    keep.wait()


def combine_kernel(arrived_ref, context_ref):
    turn = lax.rem(HD - 8 * (lax.axis_index("tp") % 16), HD)
    eight = lax.broadcasted_iota(jnp.int32, (8, HD), 1) < 8
    pieces = []
    for side in range(2):
        sources = [t for t in range(TP) if t // NEAR % 2 == side]
        levels = []
        for t in sources:
            terms = pltpu.roll(arrived_ref[t].astype(jnp.float32)[LINES:PART], turn, 1)
            terms = terms + pltpu.roll(terms, HD - 8, 1) + pltpu.roll(terms, HD - 16, 1)
            levels.append(jnp.where(eight, terms, 0.0))
        highest = levels[0]
        for level in levels[1:]:
            highest = jnp.maximum(highest, level)
        shares = [jnp.exp(level - highest) for level in levels]
        whole = shares[0]
        for share in shares[1:]:
            whole = whole + share
        scale = 1.0 / whole
        columns = jnp.transpose(jnp.concatenate([share * scale for share in shares], axis=0))
        totals = [jnp.zeros((8, HD), jnp.float32)] * QUADS
        for i, t in enumerate(sources):
            rows = arrived_ref[t].astype(jnp.float32)
            for q in range(QUADS):
                at = 8 * i + q
                totals[q] = totals[q] + columns[0:8, at : at + 1] * rows[8 * q : 8 * q + 8]
        pieces += totals
    context_ref[...] = jnp.concatenate(pieces, axis=0)


def on_device(
    hidden,
    attention_norm_scale,
    joined_projection_weight,
    adapter_down_weight,
    adapter_up_weight,
    cached_key_rows,
    cached_value_rows,
    row_adapter_index,
    lengths,
):
    width = lax.axis_size("tp")
    device = lax.axis_index("tp")
    rows_here = hidden[0]
    batch, features = rows_here.shape
    moved_rows = passed_along(rows_here, "section", 1)

    chosen = row_adapter_index[0, :, 0]
    same = chosen[:, None] == chosen[None, :]
    earlier = jnp.arange(batch)[None, :] < jnp.arange(batch)[:, None]
    place = jnp.sum(same & earlier, axis=1)
    mine = (chosen[None, :] == device) & (place[None, :] == jnp.arange(MOST)[:, None])
    slot_of_row = chosen * 8 + place * 3
    lines = slot_of_row[None, :, None] + jnp.arange(3)[:, None, None]
    spread = (lines == jnp.arange(width * 8)[None, None, :]).astype(jnp.bfloat16)

    side = device // NEAR % 2
    wide = width // NEAR
    at = [(y, z) for y in range(wide) for z in range(NEAR)]
    meetings = ([(y * NEAR + z, (y ^ 1) * NEAR + z) for y, z in at], [(y * NEAR + z, (wide - 1 - y) * NEAR + z) for y, z in at])
    given = []
    for cached in (cached_key_rows[0], cached_value_rows[0]):
        for i, pairs in enumerate(meetings):
            part = lax.dynamic_slice_in_dim(cached, SHARE * (1 - side) + GIVEN * i, GIVEN, 0)
            given.append(lax.ppermute(part, "tp", pairs))
    span = cached_key_rows.shape[2]
    own_keys = lax.dynamic_slice_in_dim(cached_key_rows[0], SHARE * side, SHARE, 0)
    copies = jnp.broadcast_to(rows_here[None], (width, batch, features))
    pieces = lax.all_to_all(copies, "tp", 0, 0)
    gathered = pieces.transpose(1, 0, 2).reshape(batch, width * features)
    wide = gathered.astype(jnp.float32)
    inverse = lax.rsqrt(jnp.mean(wide * wide, axis=-1, keepdims=True) + EPS)
    normed = (wide * inverse * attention_norm_scale).astype(jnp.bfloat16)
    shrunk = jnp.dot(normed, adapter_down_weight[0, 0], preferred_element_type=jnp.float32)
    picked = jnp.dot(
        mine.astype(jnp.bfloat16), shrunk.astype(jnp.bfloat16), preferred_element_type=jnp.float32
    ).astype(jnp.bfloat16)
    update = jnp.dot(picked, adapter_up_weight[0, 0], preferred_element_type=jnp.float32)
    columns = update.shape[1] // width
    update = (update * ADAPTER_SCALE).astype(jnp.bfloat16).reshape(MOST, width, columns)
    update = jnp.pad(update.transpose(1, 0, 2), ((0, 0), (0, 0), (0, 3 * HD - columns)))
    update = jnp.pad(update.reshape(width, 3 * MOST, HD), ((0, 0), (0, 8 - 3 * MOST), (0, 0)))
    received = lax.all_to_all(update, "tp", 0, 0)
    base = jnp.dot(normed, joined_projection_weight[0], preferred_element_type=jnp.float32)
    base = jnp.pad(base, ((0, 0), (0, 3 * HD - base.shape[1])))
    (slots,) = call(
        pack_kernel,
        4,
        (jax.ShapeDtypeStruct((TP, SLOT, HD), jnp.bfloat16),),
        [],
        base,
        spread,
        received,
        *[Far(part, pl.ANY) for part in (*given[:2], own_keys, moved_rows)],
        *[Far(part) for part in given[2:]],
    )
    joined = lax.all_to_all(slots, "tp", 0, 0)

    sent, moved_rows = call(
        attention_kernel,
        12,
        (jax.ShapeDtypeStruct((TP, PART, HD), jnp.bfloat16), pltpu.HBM((batch, features), jnp.bfloat16)),
        [
            pltpu.VMEM((TP, LINES, HD), jnp.float32),
            pltpu.VMEM((2 * KVH, LINES, HD), jnp.float32),
            pltpu.VMEM((TP, PART, HD), jnp.float32),
            pltpu.VMEM((2, 8, HD), jnp.float32),
            pltpu.VMEM((8, HD), jnp.float32),
            pltpu.VMEM((QUADS, 2 * QUAD * SPAN, HD), jnp.float32),
            pltpu.VMEM((SHARE, span, KVH * HD), jnp.bfloat16),
            pltpu.VMEM((GIVEN, span, KVH * HD), jnp.bfloat16),
            pltpu.VMEM((GIVEN, span, KVH * HD), jnp.bfloat16),
            pltpu.SemaphoreType.DMA((3,)),
            pltpu.SemaphoreType.DMA,
        ],
        joined,
        lengths,
        own_keys,
        Far(cached_value_rows[0]),
        *given[:2],
        *[Far(part) for part in given[2:]],
        moved_rows,
    )
    arrived = lax.all_to_all(sent, "tp", 0, 0)
    (context,) = call(combine_kernel, 4, (jax.ShapeDtypeStruct((ROWS * HEADS_HERE, HD), jnp.float32),), [], arrived)
    context = context.reshape(batch, HEADS_HERE * HD).astype(jnp.bfloat16)
    moved_context = passed_along(context, "section", 1)
    return (moved_rows[None], moved_context[None])


def solution(mesh):
    return jax.shard_map(
        on_device,
        mesh=mesh,
        in_specs=(
            P("section", None, "tp"),
            P(),
            P("section", None, "tp"),
            P("section", "tp", None, None),
            P("section", "tp", None, None),
            P("section", None, "tp", None),
            P("section", None, "tp", None),
            P("section", None, None),
            P("section", None),
        ),
        out_specs=(P("section", None, "tp"), P("section", None, "tp")),
        check_vma=False,
    )
```
